128 devices in a mesh: fsdp: 4 (over y_lo, core), context: 8 (over x, y_hi), tensor: 4 (over z).
Axes of the slice: x: 4, y: 4 (y_hi: 2, y_lo: 2; y = y_hi * 2 + y_lo), z: 4, core: 2. Of those that a mesh axis runs over, the one named last changes fastest.
Arguments:
- tokens: bfloat16 [4, 2048, 1152], P('fsdp', 'context'), may hold values from -6 to 6
- block_order: int32 [4, 16], P('fsdp'), may hold values from 0 to 15, each once within a row
- cotangent: bfloat16 [4, 2048, 1152], P('fsdp', 'context'), may hold values from -6 to 6
- w_query: bfloat16 [1152, 1024], P('fsdp', 'tensor'), may hold values from -0.1875 to 0.1875
- w_key: bfloat16 [1152, 256], P('fsdp'), may hold values from -0.1875 to 0.1875
- w_value: bfloat16 [1152, 256], P('fsdp'), may hold values from -0.1875 to 0.1875
- w_out: bfloat16 [1024, 1152], P('tensor', 'fsdp'), may hold values from -0.1875 to 0.1875
- w_gate: bfloat16 [1152, 6912], P('fsdp', 'tensor'), may hold values from -0.1875 to 0.1875
- w_up: bfloat16 [1152, 6912], P('fsdp', 'tensor'), may hold values from -0.1875 to 0.1875
- w_down: bfloat16 [6912, 1152], P('tensor', 'fsdp'), may hold values from -0.078125 to 0.078125
- gains: bfloat16 [4, 1152], P(None, 'fsdp'), may hold values from 0.5 to 1.5
- head_gains: bfloat16 [2, 256], P(None, 'fsdp'), may hold values from 0.5 to 1.5
Outputs:
- out: bfloat16 [4, 2048, 1152], P('fsdp', 'context')
- grad_tokens: float32 [4, 2048, 1152], P('fsdp', 'context')
- grad_w_query: float32 [1152, 1024], P('fsdp', 'tensor')
- grad_w_key: float32 [1152, 256], P('fsdp')
- grad_w_value: float32 [1152, 256], P('fsdp')
- grad_w_out: float32 [1024, 1152], P('tensor', 'fsdp')
- grad_w_gate: float32 [1152, 6912], P('fsdp', 'tensor')
- grad_w_up: float32 [1152, 6912], P('fsdp', 'tensor')
- grad_w_down: float32 [6912, 1152], P('tensor', 'fsdp')
- grad_gains: float32 [4, 1152], P(None, 'fsdp')
- grad_head_gains: float32 [2, 256], P(None, 'fsdp')
The draws below stay inside these ranges and needn't reach their ends.
Inputs may be any that keep to these rules, and one draw needn't show every extreme that they name: `block_order`: each row lists every block number of its sequence once, in a seeded order.
All inputs are finite; a program needn't handle non-finite values.
Results may differ from the reference program's by a relative error of at most 0.03.
Values may be sent and summed in bfloat16 or wider, within the bound.
A program may use at most 128 MiB of HBM per device.

```python
import math
import jax
import jax.numpy as jnp
from jax import lax

D = 1152
FF = 6912
HEADS = 4
HD = 256
LENGTH = 2048
SEQS = 4
N_CONTEXT = 8


def levels(key, extent, split, smallest, high):
    level = 1.0
    for dim, parts in split:
        steps = jax.random.uniform(jax.random.fold_in(jax.random.fold_in(key, 6), dim), (parts,), jnp.float32, smallest / len(split), high / len(split))
        level = level * jnp.repeat(jnp.exp(steps), extent[dim] // parts).reshape((-1,) + (1,) * (len(extent) - 1 - dim))
    return level


def scatter_about(own_key, dims, scale, most, shards=(), held_as=jnp.bfloat16):
    drawn = scale * jax.random.normal(own_key, dims, jnp.float32)
    if shards:
        drawn = drawn * levels(own_key, dims, shards, -0.22, 0.18)
    return jnp.clip(drawn, -most, most).astype(held_as)


def setup_inputs(seed: int = 0) -> dict:
    key_of = jax.random.split(jax.random.key(seed), 13)
    return {
        "tokens": scatter_about(key_of[0], (SEQS, LENGTH, D), 1.0, 6.0, ((0, 4), (1, 8))),
        "block_order": jax.vmap(lambda own: jax.random.permutation(own, 2 * N_CONTEXT))(jax.random.split(key_of[1], SEQS)).reshape((SEQS, 2 * N_CONTEXT)).astype(jnp.int32),
        "cotangent": scatter_about(key_of[2], (SEQS, LENGTH, D), 1.0, 6.0, ((0, 4), (1, 8))),
        "w_query": scatter_about(key_of[3], (D, HEADS * HD), D ** -0.5, 0.1875, ((0, 4), (1, 4))),
        "w_key": scatter_about(key_of[4], (D, HD), D ** -0.5, 0.1875, ((0, 4),)),
        "w_value": scatter_about(key_of[5], (D, HD), D ** -0.5, 0.1875, ((0, 4),)),
        "w_out": scatter_about(key_of[6], (HEADS * HD, D), (HEADS * HD) ** -0.5, 0.1875, ((0, 4), (1, 4))),
        "w_gate": scatter_about(key_of[7], (D, FF), D ** -0.5, 0.1875, ((0, 4), (1, 4))),
        "w_up": scatter_about(key_of[8], (D, FF), D ** -0.5, 0.1875, ((0, 4), (1, 4))),
        "w_down": scatter_about(key_of[9], (FF, D), FF ** -0.5, 0.078125, ((0, 4), (1, 4))),
        "gains": jnp.clip(1.0 + 0.1 * jax.random.normal(key_of[10], (4, D), jnp.float32), 0.5, 1.5).astype(jnp.bfloat16),
        "head_gains": jnp.clip(1.0 + 0.1 * jax.random.normal(key_of[11], (2, HD), jnp.float32), 0.5, 1.5).astype(jnp.bfloat16),
    }


@jax.custom_vjp
def low(v):
    return lax.optimization_barrier(v.astype(jnp.bfloat16)).astype(jnp.float32)

@jax.custom_vjp
def low_back(v):
    return v

def low_keep(v):
    return (low(v), None)

def low_pass(kept, grad):
    return (grad,)

def back_keep(v):
    return (v, None)

def back_low(kept, grad):
    return (low(grad),)
low.defvjp(low_keep, low_pass)
low_back.defvjp(back_keep, back_low)
ROPE_BASE = 1000000.0
EPS = 1e-06
HIGH = lax.Precision.HIGHEST

def matmul(left, right):
    return jnp.dot(left, right, precision=HIGH, preferred_element_type=jnp.float32)

def normalize(values, gain):
    return values * lax.rsqrt(lax.optimization_barrier(jnp.mean(values * values, axis=-1, keepdims=True)) + EPS) * gain

def rotate(values, cosine, sine):
    middle = values.shape[-1] // 2
    first = values[..., :middle]
    second = values[..., middle:]
    return jnp.concatenate([first * cosine - second * sine, second * cosine + first * sine], axis=-1)

def tables(positions):
    steps = jnp.arange(HD // 2, dtype=jnp.float32) * (2.0 / HD)
    inverse = jnp.exp(-math.log(ROPE_BASE) * steps)
    angle = positions.astype(jnp.float32)[:, None] * inverse[None, :]
    return (jnp.cos(angle), jnp.sin(angle))

def layer(stream, positions, w_query, w_key, w_value, w_out, w_gate, w_up, w_down, gains, head_gains):
    seq_len = stream.shape[0]
    scale = HD ** (-0.5)
    normed = low(normalize(stream, gains[0]))
    q_proj = low_back(matmul(normed, w_query)).reshape(seq_len, HEADS, HD)
    k_proj = low_back(matmul(normed, w_key))
    values = low(low_back(matmul(normed, w_value)))
    cosine, sine = tables(positions)
    queries = low(rotate(normalize(q_proj, head_gains[0]), cosine[:, None, :], sine[:, None, :]))
    keys = low(rotate(normalize(k_proj, head_gains[1]), cosine, sine))
    qblock = min(512, seq_len)

    def attend(item):
        q_block, pos_block = item
        scores = low_back(jnp.einsum('qhd,kd->qhk', q_block, keys, precision=HIGH) * scale)
        visible = positions[None, None, :] <= pos_block[:, None, None]
        top = lax.optimization_barrier(jnp.max(jnp.where(visible, scores, -1e+30), axis=-1, keepdims=True))
        total = lax.optimization_barrier(jnp.sum(jnp.where(visible, jnp.exp(scores - top), 0.0), axis=-1, keepdims=True))
        lse = top + jnp.log(total)
        probs = low(jnp.where(visible, jnp.exp(scores - lse), 0.0))
        return low(low_back(jnp.einsum('qhk,kd->qhd', probs, values, precision=HIGH)))
    attn = lax.map(jax.checkpoint(attend), (queries.reshape(-1, qblock, HEADS, HD), positions.reshape(-1, qblock)))
    attn = attn.reshape(seq_len, HEADS * HD)
    branch = low_back(matmul(attn, w_out))
    middle = stream + normalize(branch, gains[1])
    normed_two = low(normalize(middle, gains[2]))
    gate = low_back(matmul(normed_two, w_gate))
    up_part = low_back(matmul(normed_two, w_up))
    hidden = low(jax.nn.gelu(gate, approximate=True) * up_part)
    ffn = low_back(matmul(hidden, w_down))
    return middle + normalize(ffn, gains[3])

def reference(tokens, block_order, cotangent, w_query, w_key, w_value, w_out, w_gate, w_up, w_down, gains, head_gains):
    span = LENGTH // (2 * N_CONTEXT)
    offsets = jnp.arange(LENGTH, dtype=jnp.int32)
    positions = (jnp.repeat(block_order, span, axis=1) * span + (offsets % span)[None, :]).astype(jnp.int32)
    weights = tuple((weight.astype(jnp.float32) for weight in (w_query, w_key, w_value, w_out, w_gate, w_up, w_down, gains, head_gains)))

    def forward(stream, *params):

        def single(item):
            return layer(item[0], item[1], *params)
        return lax.map(single, (stream, positions))
    output, pull = jax.vjp(forward, tokens.astype(jnp.float32), *weights)
    grads = pull(cotangent.astype(jnp.float32))
    return (output.astype(jnp.bfloat16), grads[0], grads[1], grads[2], grads[3], grads[4], grads[5], grads[6], grads[7], grads[8], grads[9])
```

```python
import functools
import math

import jax
import jax.numpy as jnp
from jax import lax
from jax.experimental import pallas as pl
from jax.experimental.pallas import tpu as pltpu
from jax.sharding import PartitionSpec as P

HD = 256
ROPE_BASE = 1000000.0
EPS = 1e-06
MESH = pl.DeviceIdType.MESH
BF = jnp.bfloat16
F32 = jnp.float32


def normalize(values, gain):
    return values * lax.rsqrt(jnp.mean(values * values, axis=-1, keepdims=True) + EPS) * gain


def rotate(values, cosine, sine):
    middle = values.shape[-1] // 2
    first = values[..., :middle]
    second = values[..., middle:]
    return jnp.concatenate(
        [first * cosine - second * sine, second * cosine + first * sine], axis=-1
    )


def tables(positions):
    steps = jnp.arange(HD // 2, dtype=jnp.float32) * (2.0 / HD)
    inverse = jnp.exp(-math.log(ROPE_BASE) * steps)
    angle = positions.astype(jnp.float32)[:, None] * inverse[None, :]
    return (jnp.cos(angle), jnp.sin(angle))


def plain(left, right):
    return jnp.dot(left, right, preferred_element_type=jnp.float32)


def inner(left, right):
    return lax.dot_general(
        left, right, (((0,), (0,)), ((), ())), preferred_element_type=jnp.float32
    )


def against(left, right):
    return lax.dot_general(
        left, right, (((1,), (1,)), ((), ())), preferred_element_type=jnp.float32
    )


class Place:
    def __init__(self):
        f = lax.axis_index("fsdp")
        c = lax.axis_index("context")
        self.f, self.c, self.z = f, c, lax.axis_index("tensor")
        self.ylo, self.core = f // 2, f % 2
        self.x, self.yhi = c // 2, c % 2
        self.y = self.yhi * 2 + self.ylo

    def at(self, x=None, y=None, z=None, core=None):
        x = self.x if x is None else x
        y = self.y if y is None else y
        z = self.z if z is None else z
        core = self.core if core is None else core
        return ((y % 2) * 2 + core, x * 2 + y // 2, z)

    def sib(self):
        return self.at(core=1 - self.core)

    def dy(self, d):
        return self.at(y=(self.y + d) % 4)

    def dx(self, d):
        return self.at(x=(self.x + d) % 4)

    def dz(self, d):
        return self.at(z=(self.z + d) % 4)

    def dc(self, d):
        return (self.f, (self.c + d) % 8, self.z)

    def dcz(self, d):
        to = (self.c * 4 + self.z + d) % 32
        return (self.f, to // 4, to % 4)


def greet(devices):
    barrier = pltpu.get_barrier_semaphore()
    for device in devices:
        pl.semaphore_signal(barrier, inc=1, device_id=device, device_id_type=MESH)
    pl.semaphore_wait(barrier, len(devices))


def send(src, dst, ssem, rsem, device):
    copy = pltpu.make_async_remote_copy(
        src_ref=src, dst_ref=dst, send_sem=ssem, recv_sem=rsem, device_id=device, device_id_type=MESH
    )
    copy.start()
    return copy


def sems(n):
    return [pltpu.SemaphoreType.DMA((n,)), pltpu.SemaphoreType.DMA((n,))]


VM = pl.BlockSpec(memory_space=pltpu.VMEM)


def params(cid, limit=48):
    return pltpu.CompilerParams(
        collective_id=cid, has_side_effects=True, vmem_limit_bytes=limit * 2**20
    )


class Gather:
    def __init__(self, place, src, out, local, ssem, rsem, base):
        self.p, self.src, self.out = place, src, out
        self.local, self.ssem, self.rsem, self.base = local, ssem, rsem, base
        self.rows = src.shape[0]

    def start(self):
        p, rows, b = self.p, self.rows, self.base
        mine = pl.multiple_of(p.f * rows, rows)
        own = self.out.at[pl.ds(mine, rows)]
        s, r = self.ssem, self.rsem
        self.s = send(self.src, own, s.at[b + 2], r.at[b + 2], p.sib())
        self.l = pltpu.make_async_copy(self.src, own, self.local)
        self.l.start()

    def start_far(self):
        p, rows, half, b = self.p, self.rows, self.rows // 2, self.base
        first = self.out.at[pl.ds(pl.multiple_of(p.f * rows, half), half)]
        second = self.out.at[pl.ds(pl.multiple_of(p.f * rows + half, half), half)]
        s, r = self.ssem, self.rsem
        self.y = [
            send(self.src.at[pl.ds(0, half)], first, s.at[b], r.at[b], p.dy(1)),
            send(self.src.at[pl.ds(half, half)], second, s.at[b + 1], r.at[b + 1], p.dy(-1 + 4)),
        ]

    def forward(self):
        p, rows, b = self.p, self.rows, self.base
        for copy in self.y:
            copy.wait_recv()
        block = self.out.at[pl.ds(pl.multiple_of((2 * (1 - p.ylo) + p.core) * rows, rows), rows)]
        self.t = send(block, block, self.ssem.at[b + 3], self.rsem.at[b + 3], p.sib())

    def finish(self):
        self.l.wait()
        for copy in self.y:
            copy.wait_send()
        self.s.wait()
        self.t.wait()


class ZSum:
    def __init__(self, place, x, got, out, s1, r1, s2, r2):
        self.p, self.x, self.got, self.out = place, x, got, out
        self.s1, self.r1, self.s2, self.r2 = s1, r1, s2, r2

    def rows(self, block):
        return pl.ds(pl.multiple_of(block * 64, 64), 64)

    def start(self):
        p = self.p
        self.c1 = [
            send(
                self.x.at[self.rows((p.z + d) % 4)],
                self.got.at[d - 1],
                self.s1.at[d - 1],
                self.r1.at[d - 1],
                p.dz(d),
            )
            for d in (2, 1, 3)
        ]

    def middle(self):
        p = self.p
        for copy in self.c1:
            copy.wait_recv()
        own = self.rows(p.z)

        @pl.loop(0, 4)
        def _(i):
            at = pl.ds(pl.multiple_of(p.z * 64 + i * 16, 16), 16)
            to = pl.ds(pl.multiple_of(i * 16, 16), 16)
            total = self.x[at, :].astype(F32)
            for d in range(3):
                total = total + self.got[d, to, :].astype(F32)
            self.out[at, :] = total.astype(BF)

        self.c2 = [
            send(self.out.at[own], self.out.at[own], self.s2.at[d - 1], self.r2.at[d - 1], p.dz(d))
            for d in (2, 1, 3)
        ]

    def finish(self):
        for copy in self.c1:
            copy.wait_send()
        for copy in self.c2:
            copy.wait()


class Reduce:
    def __init__(self, place, out, bufs, cut, src=None, left=None, right=None):
        self.p, self.src, self.left, self.right = place, src, left, right
        self.out, self.cut = out, cut
        if src is None:
            self.sent, bufs = bufs[0], bufs[1:]
        self.r1, self.r2, self.q, self.r3, self.r4, self.r5, self.s, self.r = bufs
        self.n = out.shape[1]
        self.ns = 0

    def go(self, src, dst, device):
        i = self.ns
        self.ns += 1
        return send(src, dst, self.s.at[i], self.r.at[i], device)

    def rows(self, block):
        return pl.ds(pl.multiple_of(block * 288, 16), 288)

    def product(self, block, c0, c1):
        return plain(self.left[self.rows(block), :], self.right[:, c0:c1])

    def tiles(self):
        return [(c0, min(c0 + 256, self.n)) for c0 in range(0, self.n, 256)]

    def one(self):
        p = self.p
        if self.src is None:

            @pl.loop(0, 2)
            def _(j):
                for c0, c1 in self.tiles():
                    self.sent[j, :, c0:c1] = self.product(2 * j + 1 - p.core, c0, c1).astype(BF)

            blocks = [self.sent.at[j] for j in (0, 1)]
        else:
            blocks = [self.src.at[self.rows(2 * j + 1 - p.core)] for j in (0, 1)]
        self.c1 = [self.go(blocks[j], self.r1.at[j], p.sib()) for j in (0, 1)]

    def two(self):
        p = self.p
        for copy in self.c1:
            copy.wait_recv()
        if self.src is None:

            @pl.loop(0, 2)
            def _(j):
                for c0, c1 in self.tiles():
                    self.r1[j, :, c0:c1] = (
                        self.product(2 * j + p.core, c0, c1) + self.r1[j, :, c0:c1].astype(F32)
                    ).astype(BF)

        else:

            @pl.loop(0, 18)
            def _(i):
                at = pl.ds(pl.multiple_of(i * 16, 16), 16)
                for j in (0, 1):
                    row = pl.multiple_of((2 * j + p.core) * 288 + i * 16, 16)
                    own = self.src[pl.ds(row, 16), :]
                    self.r1[j, at, :] = (own.astype(F32) + self.r1[j, at, :].astype(F32)).astype(BF)

        far = 1 - p.ylo
        self.c2 = [
            self.go(self.r1.at[far, pl.ds(0, 144)], self.r2.at[pl.ds(0, 144)], p.dy(1)),
            self.go(self.r1.at[far, pl.ds(144, 144)], self.r2.at[pl.ds(144, 144)], p.dy(3)),
        ]

    def three(self):
        p, cut = self.p, self.cut
        for copy in self.c2:
            copy.wait_recv()
        rest = self.n - cut

        @pl.loop(0, 9)
        def _(i):
            for h in (0, 1):
                at = pl.ds(pl.multiple_of(h * 144 + i * 16, 16), 16)
                to = pl.ds(pl.multiple_of(i * 16, 16), 16)
                total = (self.r1[p.ylo, at, :].astype(F32) + self.r2[at, :].astype(F32)).astype(BF)
                self.q[2 * h, to, :] = total[:, :cut]
                if rest == cut:
                    self.q[2 * h + 1, to, :] = total[:, cut:]
                else:
                    self.q[2 * h + 1, to, :] = jnp.concatenate(
                        [total[:, cut:], jnp.zeros((16, cut - rest), BF)], axis=1
                    )

        self.c3 = [
            self.go(self.q.at[(p.x + d) % 4], self.r3.at[d - 1], p.dx(d)) for d in (2, 1, 3)
        ]

    def four(self):
        p = self.p
        for copy in self.c3:
            copy.wait_recv()

        @pl.loop(0, 9)
        def _(i):
            at = pl.ds(pl.multiple_of(i * 16, 16), 16)
            total = self.q[p.x, at, :].astype(F32)
            for d in range(3):
                total = total + self.r3[d, at, :].astype(F32)
            self.r5[0, at, :] = total.astype(BF)

        self.c4 = self.go(self.r5.at[0], self.r4, p.dy(2))

    def five(self):
        p = self.p
        self.c4.wait()

        @pl.loop(0, 9)
        def _(i):
            at = pl.ds(pl.multiple_of(i * 16, 16), 16)
            self.r4[at, :] = (self.r5[0, at, :].astype(F32) + self.r4[at, :].astype(F32)).astype(BF)

        self.c5 = [self.go(self.r4, self.r5.at[d], p.dx(d)) for d in (2, 1, 3)]

    def six(self):
        p, cut = self.p, self.cut
        rest = self.n - cut
        for copy in self.c3:
            copy.wait_send()
        for copy in self.c5:
            copy.wait_recv()
        for d in range(4):
            held = self.r4 if d == 0 else self.r5.at[d]
            quarter = (p.x + 4 - d) % 4

            @pl.loop(0, 9)
            def _(i):
                at = pl.ds(pl.multiple_of(i * 16, 16), 16)
                self.q[quarter, at, :] = held[at, :]

        @pl.loop(0, 9)
        def _(i):
            at = pl.ds(pl.multiple_of(i * 16, 16), 16)
            for h in (0, 1):
                to = pl.ds(pl.multiple_of(h * 144 + i * 16, 16), 16)
                self.out[to, :cut] = self.q[2 * h, at, :].astype(F32)
                self.out[to, cut:] = self.q[2 * h + 1, at, :rest].astype(F32)

        for copy in self.c2 + self.c5:
            copy.wait_send()


def reduce_buffers(n, cut, computed):
    bufs = [
        pltpu.VMEM((2, 288, n), BF),
        pltpu.VMEM((288, n), BF),
        pltpu.VMEM((4, 144, cut), BF),
        pltpu.VMEM((3, 144, cut), BF),
        pltpu.VMEM((144, cut), BF),
        pltpu.VMEM((4, 144, cut), BF),
    ] + sems(12)
    return [pltpu.VMEM((2, 288, n), BF)] + bufs if computed else bufs


def norm_back(v, gain, dy):
    r = lax.rsqrt(jnp.mean(v * v, axis=-1, keepdims=True) + EPS)
    gdy = gain * dy
    dv = r * gdy - v * (r * r * r * jnp.mean(gdy * v, axis=-1, keepdims=True))
    return dv, r * v * dy


def turn_back(d, cosine, sine):
    d1, d2 = d[:, :128], d[:, 128:]
    return jnp.concatenate([d1 * cosine + d2 * sine, d2 * cosine - d1 * sine], axis=1)


BACK_IN = (
    "x",
    "d_ffn_t",
    "hidden",
    "normed2_t",
    "d_gate",
    "d_up",
    "middle",
    "branch",
    "cot",
    "tokens",
    "gains",
    "dg3",
    "attn",
    "attn_low",
    "lse",
    "queries",
    "kv",
    "key_pos",
    "query_pos",
    "small",
    "normed_t",
    "q_proj",
    "k_proj",
    "heads",
    "cosine",
    "sine",
)
BACK_OUT = (
    "grad_tokens",
    "o_down",
    "o_gate",
    "o_up",
    "o_oq",
    "o_kv",
)


def back_kernel(*refs):
    n_in, n_out = len(BACK_IN), len(BACK_OUT)
    i = dict(zip(BACK_IN, refs))
    o = dict(zip(BACK_OUT, refs[n_in:]))
    rest = list(refs[n_in + n_out :])

    def take(n):
        got = rest[:n]
        del rest[:n]
        return got

    p = Place()
    scale = HD ** (-0.5)
    z1 = take(6)
    z2 = take(6)
    (extra, xgot, d_mid, d_branch, d_attn, delta, dq, parts, got) = take(9)
    (kv_low, dn_kv, acc, gt, hg, oq, tail) = take(7)
    ks, kr, ks2, kr2, xs, xr = take(6)
    down = Reduce(p, o["o_down"], take(9), 896, left=i["d_ffn_t"], right=i["hidden"])
    gate = Reduce(p, o["o_gate"], take(9), 896, left=i["normed2_t"], right=i["d_gate"])
    up = Reduce(p, o["o_up"], [down.sent] + take(8), 896, left=i["normed2_t"], right=i["d_up"])
    roq = Reduce(p, o["o_oq"], take(8), 256, src=oq)
    rkv = Reduce(p, o["o_kv"], take(8), 384, src=tail)
    first = ZSum(p, i["x"], *z1)
    x2 = first.out
    second = ZSum(p, x2, *z2)
    wq, wk, wv, wo = [slice(256 * j, 256 * j + 256) for j in range(4)]
    small = i["small"]

    greet([p.sib(), p.dy(1), p.dy(3)] + [p.dcz(d) for d in range(1, 32)])
    first.start()
    down.one()
    first.middle()
    gate.one()
    down.two()
    acc[...] = jnp.zeros_like(acc)
    gt[...] = jnp.zeros_like(gt)
    hg[...] = jnp.zeros_like(hg)
    extra[...] = jnp.zeros_like(extra)
    first.finish()

    @pl.loop(0, 16)
    def _(b):
        at = pl.ds(pl.multiple_of(b * 16, 16), 16)
        dm, dg = norm_back(
            i["middle"][at, :], i["gains"][2:3, :], first.out[at, :].astype(F32)
        )
        acc[2] += dg
        dm = dm + i["cot"][at, :].astype(F32)
        d_mid[at, :] = dm
        db, dg = norm_back(i["branch"][at, :].astype(F32), i["gains"][1:2, :], dm)
        acc[1] += dg
        d_branch[at, :] = db.astype(BF)

    d_attn[...] = plain(d_branch[...], small[:, wo]).astype(BF)
    delta[...] = jnp.sum(d_attn[...].astype(F32) * i["attn"][...], axis=-1, keepdims=True)
    dq[...] = jnp.zeros_like(dq)

    def keys_block(kb):
        k, v = i["kv"][kb, :, :HD], i["kv"][kb, :, HD:]
        scores = against(i["queries"][...], k) * scale
        seen = i["key_pos"][kb] <= i["query_pos"][...]
        probs = jnp.where(seen, jnp.exp(scores - i["lse"][...]), 0.0)
        d_probs = against(d_attn[...], v)
        ds = (probs * (d_probs - delta[...])).astype(BF)
        dq[...] += plain(ds, k)
        dk = inner(ds, i["queries"][...]) * scale
        dv = inner(probs.astype(BF), d_attn[...])
        parts[kb, :, :HD] = dk.astype(BF)
        parts[kb, :, HD:] = dv.astype(BF)

    def kv_copy(kb, d, dz, device):
        slot = (d % 8) * 4 + dz
        row = pl.ds(pl.multiple_of(((p.z + dz) % 4) * 64, 64), 64)
        return pltpu.make_async_remote_copy(
            src_ref=parts.at[kb, row],
            dst_ref=got.at[slot],
            send_sem=ks.at[slot],
            recv_sem=kr.at[slot],
            device_id=device,
            device_id_type=MESH,
        )

    @pl.loop(1, 8)
    def _(d):
        kb = (p.c + d) % 8
        keys_block(kb)
        for dz in range(4):
            kv_copy(kb, d, dz, (p.f, kb, (p.z + dz) % 4)).start()

    keys_block(p.c)
    for dz in range(1, 4):
        kv_copy(p.c, 8, dz, p.dz(dz)).start()

    @pl.loop(0, 4)
    def _(b):
        at = pl.ds(pl.multiple_of(b * 64, 64), 64)
        dn = turn_back(dq[at, :] * scale, i["cosine"][at, :], i["sine"][at, :])
        dv, dg = norm_back(i["q_proj"][at, :], i["heads"][4:5, :], dn)
        acc[3, :, :HD] += dg.reshape(4, 16, HD).sum(axis=0)
        dq[at, :] = dv

    dq_low = dq[...].astype(BF)
    x2[...] = against(dq_low, small[:, wq]).astype(BF)
    extra[0:1, :] = jnp.sum(acc[3, :, :HD], axis=0, keepdims=True).astype(BF)
    second.start()
    more = [
        send(extra, xgot.at[d - 1], xs.at[d - 1], xr.at[d - 1], p.dz(d)) for d in (1, 2, 3)
    ]
    gate.two()
    oq[:, :HD] = plain(i["normed_t"][...], dq_low).astype(BF)
    oq[:, HD:] = inner(d_branch[...], i["attn_low"][...]).astype(BF)
    roq.one()
    for copy in down.c1:
        copy.wait_send()
    up.one()
    down.three()
    second.middle()

    for slot in range(1, 32):
        d, dz = slot // 4, slot % 4
        kv_copy(p.c, d, dz, p.dcz(slot)).wait_recv()
    own = pl.ds(pl.multiple_of(p.z * 64, 64), 64)

    @pl.loop(0, 4)
    def _(b):
        at = pl.ds(pl.multiple_of(p.z * 64 + b * 16, 16), 16)
        to = pl.ds(pl.multiple_of(b * 16, 16), 16)
        total = parts[p.c, at, :].astype(F32)
        for slot in range(1, 32):
            total = total + got[slot, to, :].astype(F32)
        kv_low[at, :] = total.astype(BF)

    kv2 = [
        send(kv_low.at[own], kv_low.at[own], ks2.at[d - 1], kr2.at[d - 1], p.dz(d))
        for d in (2, 1, 3)
    ]
    up.two()
    gate.three()
    down.four()
    for copy in kv2:
        copy.wait_recv()
    acc[3] = jnp.zeros_like(acc[3])

    @pl.loop(0, 4)
    def _(b):
        at = pl.ds(pl.multiple_of(b * 64, 64), 64)
        dn = turn_back(kv_low[at, :HD].astype(F32), i["cosine"][at, :], i["sine"][at, :])
        dv, dg = norm_back(i["k_proj"][at, :], i["heads"][5:6, :], dn)
        acc[3, :, :HD] += dg.reshape(4, 16, HD).sum(axis=0)
        dq[at, :] = dv

    dk_low = dq[...].astype(BF)
    dn_kv[...] = against(dk_low, small[:, wk]) + against(kv_low[:, HD:], small[:, wv])
    tail[:, :HD] = plain(i["normed_t"][...], dk_low).astype(BF)
    tail[:, HD : 2 * HD] = plain(i["normed_t"][...], kv_low[:, HD:]).astype(BF)
    for copy in more:
        copy.wait()
    heads = extra[0:1, :].astype(F32)
    for d in range(3):
        heads = heads + xgot[d, 0:1, :].astype(F32)
    hg[4:5, :] = heads
    hg[5:6, :] = jnp.sum(acc[3, :, :HD], axis=0, keepdims=True)
    second.finish()

    @pl.loop(0, 16)
    def _(b):
        at = pl.ds(pl.multiple_of(b * 16, 16), 16)
        dn = second.out[at, :].astype(F32) + dn_kv[at, :]
        dv, dg = norm_back(i["tokens"][at, :].astype(F32), i["gains"][0:1, :], dn)
        acc[0] += dg
        o["grad_tokens"][at, :] = d_mid[at, :] + dv

    for g in range(3):
        gt[g : g + 1, :] = jnp.sum(acc[g], axis=0, keepdims=True)
    gt[3:4, :] = i["dg3"][...]
    last = gt[...].T
    heads_t = hg[...].T
    tail[:, 2 * HD :] = last.astype(BF)
    for f in range(4):
        tail[288 * f : 288 * f + 64, 2 * HD :] = (
            last[288 * f : 288 * f + 64] + heads_t[64 * f : 64 * f + 64]
        ).astype(BF)
    rkv.one()
    roq.two()
    rkv.two()
    down.five()
    up.three()
    gate.four()
    roq.three()
    rkv.three()
    gate.five()
    up.four()
    roq.four()
    rkv.four()
    down.six()
    up.five()
    roq.five()
    rkv.five()
    gate.six()
    up.six()
    roq.six()
    rkv.six()
    for slot in range(1, 32):
        kv_copy(p.c, slot // 4, slot % 4, p.dcz(slot)).wait_send()
    for copy in kv2 + gate.c1 + up.c1 + roq.c1 + rkv.c1:
        copy.wait_send()


def back_call(ins, cid):
    def zsum():
        return [pltpu.VMEM((3, 64, 1152), BF), pltpu.VMEM((256, 1152), BF)] + sems(3) + sems(3)

    scratch = (
        zsum()
        + zsum()
        + [
            pltpu.VMEM((16, HD), BF),
            pltpu.VMEM((3, 16, HD), BF),
            pltpu.VMEM((256, 1152), F32),
            pltpu.VMEM((256, 1152), BF),
            pltpu.VMEM((256, HD), BF),
            pltpu.VMEM((256, 1), F32),
            pltpu.VMEM((256, HD), F32),
            pltpu.VMEM((8, 256, 2 * HD), BF),
            pltpu.VMEM((32, 64, 2 * HD), BF),
            pltpu.VMEM((256, 2 * HD), BF),
            pltpu.VMEM((256, 1152), F32),
            pltpu.VMEM((4, 16, 1152), F32),
            pltpu.VMEM((128, 1152), F32),
            pltpu.VMEM((128, HD), F32),
            pltpu.VMEM((1152, 512), BF),
            pltpu.VMEM((1152, 640), BF),
        ]
        + sems(32)
        + sems(3)
        + sems(3)
        + reduce_buffers(1728, 896, True) * 2
        + reduce_buffers(1728, 896, False)
        + reduce_buffers(512, 256, False)
        + reduce_buffers(640, 384, False)
    )
    shapes = [(256, 1152)] + [(288, n) for n in (1728, 1728, 1728, 512, 640)]
    return pl.pallas_call(
        back_kernel,
        out_shape=[jax.ShapeDtypeStruct(s, F32) for s in shapes],
        in_specs=[VM] * len(BACK_IN),
        out_specs=[VM] * len(shapes),
        scratch_shapes=scratch,
        compiler_params=params(cid, 62),
        name="backward",
    )(*[ins[name] for name in BACK_IN])


FORE_IN = (
    "tokens",
    "cot",
    "small",
    "w_gate",
    "w_up",
    "w_down",
    "cosine",
    "sine",
    "key_pos",
    "query_pos",
)
FORE_OUT = (
    "out",
    "small",
    "gains",
    "heads",
    "x",
    "d_ffn_t",
    "hidden",
    "normed2_t",
    "d_gate",
    "d_up",
    "middle",
    "branch",
    "dg3",
    "attn",
    "attn_low",
    "lse",
    "queries",
    "kv",
    "normed_t",
    "q_proj",
    "k_proj",
)
TILES = [(c0, min(c0 + 256, 1728)) for c0 in range(0, 1728, 256)]


def turn(v, cosine, sine):
    v1, v2 = v[:, :128], v[:, 128:]
    return jnp.concatenate([v1 * cosine - v2 * sine, v2 * cosine + v1 * sine], axis=1)


def transpose_into(dst, src):
    for c0 in range(0, 1152, 128):
        dst[c0 : c0 + 128, :] = src[:, c0 : c0 + 128].astype(F32).T.astype(BF)


def fore_kernel(*refs):
    n_in, n_out = len(FORE_IN), len(FORE_OUT)
    i = dict(zip(FORE_IN, refs))
    o = dict(zip(FORE_OUT, refs[n_in:]))
    rest = list(refs[n_in + n_out :])

    def take(n):
        got = rest[:n]
        del rest[:n]
        return got

    p = Place()
    scale = HD ** (-0.5)
    w_gate, w_up, w_down, act, slope, normed, d_ffn, probs, head_cols, accg = take(10)
    local, gs, gr, ks, kr, vs, vr, fs, fr = take(9)
    z1, z2 = take(6), take(6)
    part = take(1)[0]
    small = o["small"]
    first = ZSum(p, part, *z1)
    second = ZSum(p, part, *z2)
    kv = o["kv"]
    gathers = [
        Gather(p, src, dst, local.at[j], gs, gr, 4 * j)
        for j, (src, dst) in enumerate(
            [(i["small"], small), (i["w_gate"], w_gate), (i["w_up"], w_up), (i["w_down"], w_down)]
        )
    ]
    g_small, g_gate, g_up, g_down = gathers

    greet([p.sib(), p.dy(1), p.dy(3)] + [p.dc(d) for d in range(1, 8)] + [p.dz(d) for d in (1, 2, 3)])
    g_small.start()
    g_small.start_far()
    g_gate.start()
    g_up.start()
    g_down.start()
    accg[...] = jnp.zeros_like(accg)
    g_small.forward()
    g_gate.start_far()
    g_small.finish()

    o["gains"][...] = small[:, 1024:].astype(F32).T[:8, :]
    for f in range(4):
        head_cols[64 * f : 64 * f + 64, :] = small[288 * f : 288 * f + 64, 1024:].astype(F32)
    o["heads"][...] = head_cols[...].T[:8, :]

    @pl.loop(0, 16)
    def _(b):
        at = pl.ds(pl.multiple_of(b * 16, 16), 16)
        normed[at, :] = normalize(i["tokens"][at, :].astype(F32), o["gains"][0:1, :]).astype(BF)

    o["q_proj"][...] = plain(normed[...], small[:, :256])
    o["k_proj"][...] = plain(normed[...], small[:, 256:512])
    kv[p.c, :, HD:] = plain(normed[...], small[:, 512:768]).astype(BF)

    quarter = pl.ds(pl.multiple_of(p.z * 64, 64), 64)
    sent = [
        send(
            kv.at[p.c, quarter, pl.ds(HD, HD)],
            kv.at[p.c, quarter, pl.ds(HD, HD)],
            vs.at[d - 1],
            vr.at[d - 1],
            p.dc(d),
        )
        for d in range(1, 8)
    ]

    @pl.loop(0, 4)
    def _(b):
        at = pl.ds(pl.multiple_of(b * 64, 64), 64)
        n = normalize(o["k_proj"][at, :], o["heads"][5:6, :])
        kv[p.c, at, :HD] = turn(n, i["cosine"][at, :], i["sine"][at, :]).astype(BF)

    keys = kv.at[p.c, :, pl.ds(0, HD)]
    sent_k = [send(keys, keys, ks.at[d - 1], kr.at[d - 1], p.dc(d)) for d in range(1, 8)]

    @pl.loop(0, 4)
    def _(b):
        at = pl.ds(pl.multiple_of(b * 64, 64), 64)
        n = normalize(o["q_proj"][at, :], o["heads"][4:5, :])
        o["queries"][at, :] = turn(n, i["cosine"][at, :], i["sine"][at, :]).astype(BF)

    for copy in sent:
        copy.wait_recv()
    sent_z = []
    for d in range(8):
        block = kv.at[(p.c + 8 - d) % 8, quarter, pl.ds(HD, HD)]
        if d == 0:
            continue
        sent_z += [
            send(block, block, fs.at[3 * d + e - 1], fr.at[3 * d + e - 1], p.dz(e))
            for e in (2, 1, 3)
        ]
    transpose_into(o["normed_t"], normed)
    for copy in sent_k:
        copy.wait_recv()
    g_gate.forward()
    g_up.start_far()

    @pl.loop(0, 4)
    def _(b):
        at = pl.ds(pl.multiple_of(b * 64, 64), 64)
        query = o["queries"][at, :]
        seen = [i["key_pos"][kb] <= i["query_pos"][at, :] for kb in range(8)]
        scores = [against(query, kv[kb, :, :HD]) * scale for kb in range(8)]
        top = jnp.max(jnp.where(seen[0], scores[0], -1e30), axis=-1, keepdims=True)
        for kb in range(1, 8):
            top = jnp.maximum(
                top, jnp.max(jnp.where(seen[kb], scores[kb], -1e30), axis=-1, keepdims=True)
            )
        scores = [jnp.where(seen[kb], jnp.exp(scores[kb] - top), 0.0) for kb in range(8)]
        total = jnp.sum(scores[0], axis=-1, keepdims=True)
        for kb in range(1, 8):
            total = total + jnp.sum(scores[kb], axis=-1, keepdims=True)
        o["lse"][at, :] = top + jnp.log(total)
        share = 1.0 / total
        for kb in range(8):
            probs[kb, at, :] = (scores[kb] * share).astype(BF)

    for copy in sent_z:
        copy.wait_recv()
    attn = plain(probs[0], kv[0, :, HD:])
    for kb in range(1, 8):
        attn = attn + plain(probs[kb], kv[kb, :, HD:])
    o["attn"][...] = attn
    attn_low = attn.astype(BF)
    o["attn_low"][...] = attn_low
    part[...] = against(attn_low, small[:, 768:1024]).astype(BF)
    first.start()
    g_up.forward()
    g_down.start_far()
    first.middle()
    g_gate.finish()
    first.finish()

    @pl.loop(0, 16)
    def _(b):
        at = pl.ds(pl.multiple_of(b * 16, 16), 16)
        branch = first.out[at, :]
        o["branch"][at, :] = branch
        middle = i["tokens"][at, :].astype(F32) + normalize(
            branch.astype(F32), o["gains"][1:2, :]
        )
        o["middle"][at, :] = middle
        normed[at, :] = normalize(middle, o["gains"][2:3, :]).astype(BF)

    g_up.finish()
    for c0, c1 in TILES:
        gate = plain(normed[...], w_gate[:, c0:c1])
        up = plain(normed[...], w_up[:, c0:c1])
        bend = jnp.tanh(0.7978845608028654 * (gate + 0.044715 * gate * gate * gate))
        gelu = 0.5 * gate * (1.0 + bend)
        o["hidden"][:, c0:c1] = (gelu * up).astype(BF)
        act[:, c0:c1] = gelu
        rise = 0.7978845608028654 * (1.0 + 0.134145 * gate * gate)
        slope[:, c0:c1] = up * (0.5 * (1.0 + bend) + 0.5 * gate * (1.0 - bend * bend) * rise)
    g_down.forward()
    g_down.finish()
    for c0 in range(0, 1152, 384):
        part[:, c0 : c0 + 384] = against(o["hidden"][...], w_down[c0 : c0 + 384, :]).astype(BF)
    second.start()
    transpose_into(o["normed2_t"], normed)
    second.middle()
    second.finish()

    @pl.loop(0, 16)
    def _(b):
        at = pl.ds(pl.multiple_of(b * 16, 16), 16)
        ffn = second.out[at, :].astype(F32)
        o["out"][at, :] = (o["middle"][at, :] + normalize(ffn, o["gains"][3:4, :])).astype(BF)
        dv, dg = norm_back(ffn, o["gains"][3:4, :], i["cot"][at, :].astype(F32))
        accg[...] += dg
        d_ffn[at, :] = dv.astype(BF)

    o["dg3"][...] = jnp.sum(accg[...], axis=0, keepdims=True)
    transpose_into(o["d_ffn_t"], d_ffn)
    for c0, c1 in TILES:
        d_hidden = plain(d_ffn[...], w_down[:, c0:c1])
        o["d_up"][:, c0:c1] = (d_hidden * act[:, c0:c1]).astype(BF)
        o["d_gate"][:, c0:c1] = (d_hidden * slope[:, c0:c1]).astype(BF)
    for c0 in range(0, 1152, 384):
        o["x"][:, c0 : c0 + 384] = (
            against(o["d_gate"][...], w_gate[c0 : c0 + 384, :])
            + against(o["d_up"][...], w_up[c0 : c0 + 384, :])
        ).astype(BF)
    for copy in sent + sent_k + sent_z:
        copy.wait_send()


def fore_call(ins, cid):
    def zsum():
        return [pltpu.VMEM((3, 64, 1152), BF), pltpu.VMEM((256, 1152), BF)] + sems(3) + sems(3)

    scratch = (
        [pltpu.VMEM((1152, 1728), BF)] * 3
        + [
            pltpu.VMEM((256, 1728), F32),
            pltpu.VMEM((256, 1728), F32),
            pltpu.VMEM((256, 1152), BF),
            pltpu.VMEM((256, 1152), BF),
            pltpu.VMEM((8, 256, 256), BF),
            pltpu.VMEM((256, 128), F32),
            pltpu.VMEM((16, 1152), F32),
            pltpu.SemaphoreType.DMA((4,)),
        ]
        + sems(16)
        + sems(7)
        + sems(7)
        + sems(24)
        + zsum()
        + zsum()
        + [pltpu.VMEM((256, 1152), BF)]
    )
    shapes = dict(
        out=((256, 1152), BF),
        small=((1152, 1152), BF),
        gains=((8, 1152), F32),
        heads=((8, 256), F32),
        x=((256, 1152), BF),
        d_ffn_t=((1152, 256), BF),
        hidden=((256, 1728), BF),
        normed2_t=((1152, 256), BF),
        d_gate=((256, 1728), BF),
        d_up=((256, 1728), BF),
        middle=((256, 1152), F32),
        branch=((256, 1152), BF),
        dg3=((1, 1152), F32),
        attn=((256, 256), F32),
        attn_low=((256, 256), BF),
        lse=((256, 1), F32),
        queries=((256, 256), BF),
        kv=((8, 256, 512), BF),
        normed_t=((1152, 256), BF),
        q_proj=((256, 256), F32),
        k_proj=((256, 256), F32),
    )
    done = pl.pallas_call(
        fore_kernel,
        out_shape=[jax.ShapeDtypeStruct(*shapes[name]) for name in FORE_OUT],
        in_specs=[VM] * len(FORE_IN),
        out_specs=[VM] * len(FORE_OUT),
        scratch_shapes=scratch,
        compiler_params=params(cid, 62),
        name="forward",
    )(*[ins[name] for name in FORE_IN])
    return dict(zip(FORE_OUT, done))


def per_device(
    tokens,
    block_order,
    cotangent,
    w_query,
    w_key,
    w_value,
    w_out,
    w_gate,
    w_up,
    w_down,
    gains,
    head_gains,
):
    _, rows, width = tokens.shape
    cycle_index = lax.axis_index("context")
    span = rows // 2
    seq_len = rows * 8

    small = jnp.concatenate(
        [
            w_query,
            w_key,
            w_value,
            w_out.T,
            jnp.pad(
                jnp.concatenate(
                    [gains.T, jnp.pad(head_gains.T, ((0, 288 - 64), (0, 0)))], axis=1
                ),
                ((0, 0), (0, 122)),
            ),
        ],
        axis=1,
    )
    offsets = jnp.arange(seq_len, dtype=jnp.int32)
    key_pos = (jnp.repeat(block_order, span, axis=1) * span + (offsets % span)[None, :])[0]
    query_pos = lax.dynamic_slice_in_dim(key_pos, cycle_index * rows, rows, 0)
    cosine, sine = tables(query_pos)
    ins = dict(
        tokens=tokens[0],
        cot=cotangent[0],
        small=small,
        w_gate=w_gate,
        w_up=w_up,
        w_down=w_down.T,
        cosine=cosine,
        sine=sine,
        key_pos=key_pos.reshape(8, 1, rows),
        query_pos=query_pos[:, None],
    )
    held = fore_call(ins, 1)
    result = held["out"][None]
    grad_tokens, sum_down, sum_gate, sum_up, sum_oq, sum_kv = back_call({**ins, **held}, 2)
    return (
        result,
        grad_tokens[None],
        sum_oq[:, :HD],
        sum_kv[:, :HD],
        sum_kv[:, HD : 2 * HD],
        sum_oq[:, HD:].T,
        sum_gate,
        sum_up,
        sum_down.T,
        sum_kv[:, 512:516].T,
        sum_kv[:64, 516:518].T,
    )


def solution(mesh):
    in_specs = (
        P("fsdp", "context", None),
        P("fsdp", None),
        P("fsdp", "context", None),
        P("fsdp", "tensor"),
        P("fsdp", None),
        P("fsdp", None),
        P("tensor", "fsdp"),
        P("fsdp", "tensor"),
        P("fsdp", "tensor"),
        P("tensor", "fsdp"),
        P(None, "fsdp"),
        P(None, "fsdp"),
    )
    out_specs = (
        P("fsdp", "context", None),
        P("fsdp", "context", None),
        P("fsdp", "tensor"),
        P("fsdp", None),
        P("fsdp", None),
        P("tensor", "fsdp"),
        P("fsdp", "tensor"),
        P("fsdp", "tensor"),
        P("tensor", "fsdp"),
        P(None, "fsdp"),
        P(None, "fsdp"),
    )
    return jax.shard_map(
        per_device, mesh=mesh, in_specs=in_specs, out_specs=out_specs, check_vma=False
    )
```

```python
import functools
import math
from typing import Any, NamedTuple

import jax
import jax.numpy as jnp
from jax import lax
from jax.experimental import pallas as pl
from jax.experimental.pallas import tpu as pltpu
from jax.sharding import PartitionSpec as P

HD = 256
ROPE_BASE = 1000000.0
EPS = 1e-06
MESH = pl.DeviceIdType.MESH
BF = jnp.bfloat16
F32 = jnp.float32


def normalize(values, gain):
    return values * lax.rsqrt(jnp.mean(values * values, axis=-1, keepdims=True) + EPS) * gain


def rotate(values, cosine, sine):
    middle = values.shape[-1] // 2
    first = values[..., :middle]
    second = values[..., middle:]
    return jnp.concatenate(
        [first * cosine - second * sine, second * cosine + first * sine], axis=-1
    )


def tables(positions):
    steps = jnp.arange(HD // 2, dtype=jnp.float32) * (2.0 / HD)
    inverse = jnp.exp(-math.log(ROPE_BASE) * steps)
    angle = positions.astype(jnp.float32)[:, None] * inverse[None, :]
    return (jnp.cos(angle), jnp.sin(angle))


def plain(left, right):
    return jnp.dot(left, right, preferred_element_type=jnp.float32)


def inner(left, right):
    return lax.dot_general(
        left, right, (((0,), (0,)), ((), ())), preferred_element_type=jnp.float32
    )


def against(left, right):
    return lax.dot_general(
        left, right, (((1,), (1,)), ((), ())), preferred_element_type=jnp.float32
    )


class Place:
    def __init__(self):
        f = lax.axis_index("fsdp")
        c = lax.axis_index("context")
        self.f, self.c, self.z = f, c, lax.axis_index("tensor")
        self.ylo, self.core = f // 2, f % 2
        self.x, self.yhi = c // 2, c % 2
        self.y = self.yhi * 2 + self.ylo

    def at(self, x=None, y=None, z=None, core=None):
        x = self.x if x is None else x
        y = self.y if y is None else y
        z = self.z if z is None else z
        core = self.core if core is None else core
        return ((y % 2) * 2 + core, x * 2 + y // 2, z)

    def sib(self):
        return self.at(core=1 - self.core)

    def dy(self, d):
        return self.at(y=(self.y + d) % 4)

    def dx(self, d):
        return self.at(x=(self.x + d) % 4)

    def dz(self, d):
        return self.at(z=(self.z + d) % 4)

    def dc(self, d):
        return (self.f, (self.c + d) % 8, self.z)


def greet(devices):
    barrier = pltpu.get_barrier_semaphore()
    for device in devices:
        pl.semaphore_signal(barrier, inc=1, device_id=device, device_id_type=MESH)
    pl.semaphore_wait(barrier, len(devices))


def send(src, dst, ssem, rsem, device):
    copy = pltpu.make_async_remote_copy(
        src_ref=src, dst_ref=dst, send_sem=ssem, recv_sem=rsem, device_id=device, device_id_type=MESH
    )
    copy.start()
    return copy


def sems(n):
    return [pltpu.SemaphoreType.DMA((n,)), pltpu.SemaphoreType.DMA((n,))]


VM = pl.BlockSpec(memory_space=pltpu.VMEM)


def params(cid, limit=48):
    return pltpu.CompilerParams(
        collective_id=cid, has_side_effects=True, vmem_limit_bytes=limit * 2**20
    )


class Gather:
    def __init__(self, place, src, out, local, ssem, rsem, base, relay=False):
        self.p, self.src, self.out = place, src, out
        self.local, self.ssem, self.rsem, self.base = local, ssem, rsem, base
        self.rows, self.relay = src.shape[0], relay

    def go(self, n, src, dst, device):
        return send(src, dst, self.ssem.at[self.base + n], self.rsem.at[self.base + n], device)

    def at(self, row, n):
        return self.out.at[pl.ds(pl.multiple_of(row, 16), n)]

    def start(self):
        p, rows = self.p, self.rows
        own = self.at(p.f * rows, rows)
        self.s = self.go(2, self.src, own, p.sib())
        self.l = pltpu.make_async_copy(self.src, own, self.local)
        self.l.start()

    def start_far(self):
        p, rows, half = self.p, self.rows, self.rows // 2
        first, n = (64 * (p.x % 2), 80) if self.relay else (0, half)
        self.y = []
        for h, d in ((0, 1), (1, 3)):
            row = first + half * h
            src = self.src.at[pl.ds(pl.multiple_of(row, 16), n)]
            self.y.append(self.go(h, src, self.at(p.f * rows + row, n), p.dy(d)))

    def across(self):
        p, half = self.p, self.rows // 2
        for copy in self.y:
            copy.wait_recv()
        row = (2 * (1 - p.ylo) + p.core) * self.rows
        flip, back = p.x + 1 - 2 * (p.x % 2), 3 - p.x
        self.w = []
        for h, x in ((0, flip), (1, back)):
            part = self.at(row + half * h + 80 * (p.x % 2), 64)
            self.w.append(self.go(4 + h, part, part, p.at(x=x)))

    def forward(self):
        p, rows = self.p, self.rows
        for copy in self.w if self.relay else self.y:
            copy.wait_recv()
        block = self.at((2 * (1 - p.ylo) + p.core) * rows, rows)
        self.t = self.go(3, block, block, p.sib())

    def finish(self):
        self.l.wait()
        for copy in self.y:
            copy.wait_send()
        if self.relay:
            for copy in self.w:
                copy.wait_send()
        self.s.wait()
        self.t.wait()


class ZSum:
    def __init__(self, place, x, out, base, got, s1, r1, s2, r2):
        self.p, self.x, self.got, self.out = place, x, got, out
        self.base, self.share = base, got.shape[1]
        self.s1, self.r1, self.s2, self.r2 = s1, r1, s2, r2

    def rows(self, block):
        return pl.ds(pl.multiple_of(self.base + block * self.share, 32), self.share)

    def start(self):
        p = self.p
        self.c1 = [
            send(
                self.x.at[self.rows((p.z + d) % 4)],
                self.got.at[d - 1],
                self.s1.at[d - 1],
                self.r1.at[d - 1],
                p.dz(d),
            )
            for d in (2, 1, 3)
        ]

    def middle(self):
        p = self.p
        for copy in self.c1:
            copy.wait_recv()
        own = self.rows(p.z)

        @pl.loop(0, self.share // 16)
        def _(i):
            at = pl.ds(pl.multiple_of(self.base + p.z * self.share + i * 16, 16), 16)
            to = pl.ds(pl.multiple_of(i * 16, 16), 16)
            total = self.x[at, :].astype(F32)
            for d in range(3):
                total = total + self.got[d, to, :].astype(F32)
            self.out[at, :] = total.astype(BF)

        self.c2 = [
            send(self.out.at[own], self.out.at[own], self.s2.at[d - 1], self.r2.at[d - 1], p.dz(d))
            for d in (2, 1, 3)
        ]

    def finish(self):
        for copy in self.c1:
            copy.wait_send()
        for copy in self.c2:
            copy.wait()


class Reduce:
    def __init__(self, place, out, bufs, cut, src=None, left=None, right=None, direct=False):
        self.p, self.src, self.left, self.right = place, src, left, right
        self.outs, self.cut = out, cut
        if src is None:
            self.sent, bufs = bufs[0], bufs[1:]
        self.r1, self.r2, self.q, self.r3, self.r4, self.r5, self.r6, self.s, self.r = bufs
        self.n = sum(ref.shape[1] for ref in out)
        self.ns, self.direct = 0, direct
        x, side = place.x, (cut // 128 + 1) // 2 * 128
        flip, back = x + 1 - 2 * (x % 2), 3 - x
        self.ways = [
            (flip, back, 3 - flip, pl.ds(0, side)),
            (back, flip, back + 1 - 2 * (back % 2), pl.ds(side, cut - side)),
        ]

    def go(self, src, dst, device):
        i = self.ns
        self.ns += 1
        return send(src, dst, self.s.at[i], self.r.at[i], device)

    def rows(self, block):
        return pl.ds(pl.multiple_of(block * 288, 16), 288)

    def product(self, block, c0, c1):
        return plain(self.left[self.rows(block), :], self.right[:, c0:c1])

    def tiles(self):
        return [(c0, min(c0 + 256, self.n)) for c0 in range(0, self.n, 256)]

    def one(self):
        p = self.p
        if self.src is None:

            @pl.loop(0, 2)
            def _(j):
                for c0, c1 in self.tiles():
                    self.sent[j, :, c0:c1] = self.product(2 * j + 1 - p.core, c0, c1).astype(BF)

            blocks = [self.sent.at[j] for j in (0, 1)]
        else:
            blocks = [self.src.at[self.rows(2 * j + 1 - p.core)] for j in (0, 1)]
        self.c1 = [self.go(blocks[j], self.r1.at[j], p.sib()) for j in (0, 1)]

    def two(self):
        p = self.p
        for copy in self.c1:
            copy.wait_recv()
        if self.src is None:

            @pl.loop(0, 2)
            def _(j):
                for c0, c1 in self.tiles():
                    self.r1[j, :, c0:c1] = (
                        self.product(2 * j + p.core, c0, c1) + self.r1[j, :, c0:c1].astype(F32)
                    ).astype(BF)

        else:

            @pl.loop(0, 18)
            def _(i):
                at = pl.ds(pl.multiple_of(i * 16, 16), 16)
                for j in (0, 1):
                    row = pl.multiple_of((2 * j + p.core) * 288 + i * 16, 16)
                    own = self.src[pl.ds(row, 16), :]
                    self.r1[j, at, :] = (own.astype(F32) + self.r1[j, at, :].astype(F32)).astype(BF)

        far = 1 - p.ylo
        self.c2 = [
            self.go(self.r1.at[far, pl.ds(0, 144)], self.r2.at[pl.ds(0, 144)], p.dy(1)),
            self.go(self.r1.at[far, pl.ds(144, 144)], self.r2.at[pl.ds(144, 144)], p.dy(3)),
        ]

    def three(self):
        p, cut = self.p, self.cut
        for copy in self.c2:
            copy.wait_recv()
        rest = self.n - cut

        @pl.loop(0, 9)
        def _(i):
            for h in (0, 1):
                at = pl.ds(pl.multiple_of(h * 144 + i * 16, 16), 16)
                to = pl.ds(pl.multiple_of(i * 16, 16), 16)
                total = (self.r1[p.ylo, at, :].astype(F32) + self.r2[at, :].astype(F32)).astype(BF)
                self.q[2 * h, to, :] = total[:, :cut]
                if rest == cut:
                    self.q[2 * h + 1, to, :] = total[:, cut:]
                else:
                    self.q[2 * h + 1, to, :] = jnp.concatenate(
                        [total[:, cut:], jnp.zeros((16, cut - rest), BF)], axis=1
                    )

        if self.direct:
            self.c3 = [
                self.go(self.q.at[(p.x + d) % 4], self.r3.at[d - 1], p.dx(d)) for d in (2, 1, 3)
            ]
            return
        self.c3 = []
        for one, two, theirs, cols in self.ways:
            for k, quarter in enumerate((one, theirs)):
                self.c3.append(
                    self.go(self.q.at[quarter, :, cols], self.r3.at[k, :, cols], p.at(x=one))
                )

    def sum_rows(self, dst, first, *more):
        @pl.loop(0, 9)
        def _(i):
            at = pl.ds(pl.multiple_of(i * 16, 16), 16)
            total = first[at, :].astype(F32)
            for ref in more:
                total = total + ref[at, :].astype(F32)
            dst[at, :] = total.astype(BF)

    def four(self):
        p = self.p
        for copy in self.c3:
            copy.wait_recv()
        if self.direct:
            return
        mine = self.q.at[p.x]
        self.sum_rows(mine, mine, self.r3.at[0])
        self.c3b = []
        for one, two, _, cols in self.ways:
            held = self.q.at[two, :, cols]
            self.sum_rows(held, held, self.r3.at[1, :, cols])
            self.c3b.append(self.go(held, self.r3.at[2, :, cols], p.at(x=two)))

    def fourb(self):
        p = self.p
        if self.direct:
            self.sum_rows(self.r6, self.q.at[p.x], *[self.r3.at[d] for d in range(3)])
        else:
            for copy in self.c3b:
                copy.wait_recv()
            self.sum_rows(self.r6, self.q.at[p.x], self.r3.at[2])
        self.c4 = self.go(self.r6, self.r4, p.dy(2))

    def five(self):
        p = self.p
        self.c4.wait()
        mine = self.r5.at[p.x]
        self.sum_rows(mine, self.r6, self.r4)
        if self.direct:
            self.c5 = [self.go(mine, mine, p.dx(d)) for d in (2, 1, 3)]
            return
        self.c5 = []
        for one, two, _, cols in self.ways:
            part = self.r5.at[p.x, :, cols]
            self.c5.append(self.go(part, part, p.at(x=two)))
            self.c5.append(self.go(part, part, p.at(x=one)))

    def fiveb(self):
        p = self.p
        self.c5b = []
        if self.direct:
            return
        for k, (one, two, _, cols) in enumerate(self.ways):
            self.c5[2 * k].wait_recv()
            part = self.r5.at[two, :, cols]
            self.c5b.append(self.go(part, part, p.at(x=one)))

    def put(self, rows, c0, value):
        start = 0
        for ref in self.outs:
            end = start + ref.shape[1]
            lo, hi = max(c0, start), min(c0 + value.shape[1], end)
            if lo < hi:
                ref[rows, lo - start : hi - start] = value[:, lo - c0 : hi - c0]
            start = end

    def six(self):
        rest = self.n - self.cut
        for copy in self.c5b + (self.c5 if self.direct else self.c5[1::2]):
            copy.wait_recv()

        @pl.loop(0, 9)
        def _(i):
            at = pl.ds(pl.multiple_of(i * 16, 16), 16)
            for h in (0, 1):
                to = pl.ds(pl.multiple_of(h * 144 + i * 16, 16), 16)
                self.put(to, 0, self.r5[2 * h, at, :])
                self.put(to, self.cut, self.r5[2 * h + 1, at, :rest])

        for copy in self.c2 + self.c3 + self.c5 + self.c5b:
            copy.wait_send()
        if not self.direct:
            for copy in self.c3b:
                copy.wait_send()


def reduce_buffers(n, cut, computed):
    bufs = [
        pltpu.VMEM((2, 288, n), BF),
        pltpu.VMEM((288, n), BF),
        pltpu.VMEM((4, 144, cut), BF),
        pltpu.VMEM((3, 144, cut), BF),
        pltpu.VMEM((144, cut), BF),
        pltpu.VMEM((4, 144, cut), BF),
        pltpu.VMEM((144, cut), BF),
    ] + sems(20)
    return [pltpu.VMEM((2, 288, n), BF)] + bufs if computed else bufs


def norm_back(v, gain, dy):
    r = lax.rsqrt(jnp.mean(v * v, axis=-1, keepdims=True) + EPS)
    gdy = gain * dy
    dv = r * gdy - v * (r * r * r * jnp.mean(gdy * v, axis=-1, keepdims=True))
    return dv, r * v * dy


def turn_back(d, cosine, sine):
    d1, d2 = d[:, :128], d[:, 128:]
    return jnp.concatenate([d1 * cosine + d2 * sine, d2 * cosine - d1 * sine], axis=1)


class BackIn(NamedTuple):
    x: Any
    d_ffn_t: Any
    hidden: Any
    normed2_t: Any
    d_gate: Any
    d_up: Any
    middle: Any
    branch: Any
    cot: Any
    tokens: Any
    gains: Any
    dg3: Any
    attn: Any
    attn_low: Any
    lse: Any
    queries: Any
    kv: Any
    key_pos: Any
    query_pos: Any
    small: Any
    normed_t: Any
    q_proj: Any
    k_proj: Any
    heads: Any
    cosine: Any
    sine: Any

class BackOut(NamedTuple):
    grad_tokens: Any
    o_down: Any
    o_gate: Any
    o_up: Any
    o_q: Any
    o_o: Any
    o_k: Any
    o_v: Any
    o_last: Any


def back_kernel(*refs):
    n_in, n_out = len(BackIn._fields), len(BackOut._fields)
    i = BackIn(*refs[:n_in])
    o = BackOut(*refs[n_in : n_in + n_out])
    rest = list(refs[n_in + n_out :])

    def take(n):
        got = rest[:n]
        del rest[:n]
        return got

    p = Place()
    scale = HD ** (-0.5)
    total1 = take(1)[0]
    z1 = take(10)
    total2 = take(1)[0]
    z2 = take(5)
    (extra, xgot, d_mid, d_branch, d_attn, delta, dq, parts) = take(8)
    got_k, got_v, k_sum, v_sum, far_k, far_v = take(6)
    (kv_low, dn_kv, acc, gt, hg, oq, tail) = take(7)
    ks, kr, vs, vr, ks2, kr2, vs2, vr2, os, orr, xs, xr = take(12)
    down = Reduce(p, [o.o_down], take(10), 896, left=i.d_ffn_t, right=i.hidden)
    gate = Reduce(p, [o.o_gate], take(10), 896, left=i.normed2_t, right=i.d_gate)
    up = Reduce(p, [o.o_up], [down.sent] + take(9), 896, left=i.normed2_t, right=i.d_up)
    roq = Reduce(p, [o.o_q, o.o_o], take(9), 256, src=oq)
    rkv = Reduce(p, [o.o_k, o.o_v, o.o_last], take(9), 384, src=tail, direct=True)
    firsts = [ZSum(p, i.x, total1, 128 * h, *z1[5 * h : 5 * h + 5]) for h in (0, 1)]
    x2 = total1
    second = ZSum(p, x2, total2, 0, *z2)
    wq, wk, wv, wo = [slice(256 * j, 256 * j + 256) for j in range(4)]
    small = i.small

    greet(
        [p.sib(), p.dy(1), p.dy(3)]
        + [p.dc(d) for d in range(1, 8)]
        + [p.dz(d) for d in (1, 2, 3)]
    )
    for half in firsts:
        half.start()
    down.one()
    gate.one()
    acc[...] = jnp.zeros_like(acc)
    gt[...] = jnp.zeros_like(gt)
    hg[...] = jnp.zeros_like(hg)
    extra[...] = jnp.zeros_like(extra)
    firsts[0].middle()
    down.two()
    firsts[1].middle()
    gate.two()
    for copy in down.c1:
        copy.wait_send()
    up.one()
    for half in firsts:
        half.finish()

    @pl.loop(0, 16)
    def _(b):
        at = pl.ds(pl.multiple_of(b * 16, 16), 16)
        dm, dg = norm_back(
            i.middle[at, :], i.gains[2:3, :], total1[at, :].astype(F32)
        )
        acc[2] += dg
        dm = dm + i.cot[at, :].astype(F32)
        d_mid[at, :] = dm
        db, dg = norm_back(i.branch[at, :].astype(F32), i.gains[1:2, :], dm)
        acc[1] += dg
        d_branch[at, :] = db.astype(BF)

    down.three()
    d_attn[...] = plain(d_branch[...], small[:, wo]).astype(BF)
    delta[...] = jnp.sum(d_attn[...].astype(F32) * i.attn[...], axis=-1, keepdims=True)
    dq[...] = jnp.zeros_like(dq)
    up.two()

    def keys_block(kb):
        k, v = i.kv[kb, :, :HD], i.kv[kb, :, HD:]
        scores = against(i.queries[...], k) * scale
        seen = i.key_pos[kb] <= i.query_pos[...]
        probs = jnp.where(seen, jnp.exp(scores - i.lse[...]), 0.0)
        d_probs = against(d_attn[...], v)
        ds = (probs * (d_probs - delta[...])).astype(BF)
        dq[...] += plain(ds, k)
        dk = inner(ds, i.queries[...]) * scale
        dv = inner(probs.astype(BF), d_attn[...])
        parts[kb, :, :HD] = dk.astype(BF)
        parts[kb, :, HD:] = dv.astype(BF)

    def key_copy(kb, d, e):
        slot = 3 * (d % 8) + e - 1
        row = pl.ds(pl.multiple_of(((p.z + e) % 4) * 64, 64), 64)
        return pltpu.make_async_remote_copy(
            src_ref=parts.at[kb, row, pl.ds(0, HD)],
            dst_ref=got_k.at[e - 1, d % 8],
            send_sem=ks.at[slot],
            recv_sem=kr.at[slot],
            device_id=p.dz(e),
            device_id_type=MESH,
        )

    def value_copy(kb, d):
        return pltpu.make_async_remote_copy(
            src_ref=parts.at[kb, :, pl.ds(HD, HD)],
            dst_ref=got_v.at[d - 1],
            send_sem=vs.at[d - 1],
            recv_sem=vr.at[d - 1],
            device_id=(p.f, kb, p.z),
            device_id_type=MESH,
        )

    @pl.loop(1, 8)
    def _(d):
        kb = (p.c + d) % 8
        keys_block(kb)
        value_copy(kb, d).start()
        for e in (2, 1, 3):
            key_copy(kb, d, e).start()

    keys_block(p.c)
    for e in (2, 1, 3):
        key_copy(p.c, 0, e).start()

    gate.three()

    @pl.loop(0, 4)
    def _(b):
        at = pl.ds(pl.multiple_of(b * 64, 64), 64)
        dn = turn_back(dq[at, :] * scale, i.cosine[at, :], i.sine[at, :])
        dv, dg = norm_back(i.q_proj[at, :], i.heads[4:5, :], dn)
        acc[3, :, :HD] += dg.reshape(4, 16, HD).sum(axis=0)
        dq[at, :] = dv

    dq_low = dq[...].astype(BF)
    x2[...] = against(dq_low, small[:, wq]).astype(BF)
    extra[0:1, :] = jnp.sum(acc[3, :, :HD], axis=0, keepdims=True).astype(BF)
    second.start()
    more = [
        send(extra, xgot.at[d - 1], xs.at[d - 1], xr.at[d - 1], p.dz(d)) for d in (1, 2, 3)
    ]
    oq[:, :HD] = plain(i.normed_t[...], dq_low).astype(BF)
    oq[:, HD:] = inner(d_branch[...], i.attn_low[...]).astype(BF)
    roq.one()
    down.four()

    for d in range(8):
        for e in (1, 2, 3):
            key_copy(p.c, d, e).wait_recv()
    own = pl.ds(pl.multiple_of(p.z * 64, 64), 64)

    @pl.loop(0, 8)
    def _(d):
        kb = (p.c + d) % 8
        total = parts[kb, own, :HD].astype(F32)
        for e in range(3):
            total = total + got_k[e, d].astype(F32)
        k_sum[d] = total.astype(BF)

    keys_far = [
        send(k_sum.at[d], far_k.at[d - 1], ks2.at[d - 1], kr2.at[d - 1], p.dc(d))
        for d in range(1, 8)
    ]
    for d in range(1, 8):
        value_copy(p.c, d).wait_recv()

    @pl.loop(0, 16)
    def _(b):
        at = pl.ds(pl.multiple_of(b * 16, 16), 16)
        total = parts[p.c, at, HD:].astype(F32)
        for d in range(7):
            total = total + got_v[d, at, :].astype(F32)
        v_sum[at, :] = total.astype(BF)

    values_far = [
        send(
            v_sum.at[pl.ds(pl.multiple_of(((p.z + e) % 4) * 64, 64), 64)],
            far_v.at[e - 1],
            vs2.at[e - 1],
            vr2.at[e - 1],
            p.dz(e),
        )
        for e in (2, 1, 3)
    ]
    second.middle()
    down.fourb()
    up.three()
    gate.four()
    for copy in keys_far + values_far:
        copy.wait_recv()

    @pl.loop(0, 4)
    def _(b):
        at = pl.ds(pl.multiple_of(p.z * 64 + b * 16, 16), 16)
        to = pl.ds(pl.multiple_of(b * 16, 16), 16)
        total = k_sum[0, to, :].astype(F32)
        for d in range(7):
            total = total + far_k[d, to, :].astype(F32)
        kv_low[at, :HD] = total.astype(BF)
        total = v_sum[at, :].astype(F32)
        for e in range(3):
            total = total + far_v[e, to, :].astype(F32)
        kv_low[at, HD:] = total.astype(BF)

    kv2 = [
        send(kv_low.at[own], kv_low.at[own], os.at[d - 1], orr.at[d - 1], p.dz(d))
        for d in (2, 1, 3)
    ]
    down.five()
    roq.two()
    for copy in kv2:
        copy.wait_recv()
    acc[3] = jnp.zeros_like(acc[3])

    @pl.loop(0, 4)
    def _(b):
        at = pl.ds(pl.multiple_of(b * 64, 64), 64)
        dn = turn_back(kv_low[at, :HD].astype(F32), i.cosine[at, :], i.sine[at, :])
        dv, dg = norm_back(i.k_proj[at, :], i.heads[5:6, :], dn)
        acc[3, :, :HD] += dg.reshape(4, 16, HD).sum(axis=0)
        dq[at, :] = dv

    dk_low = dq[...].astype(BF)
    dn_kv[...] = against(dk_low, small[:, wk]) + against(kv_low[:, HD:], small[:, wv])
    tail[:, :HD] = plain(i.normed_t[...], dk_low).astype(BF)
    tail[:, HD : 2 * HD] = plain(i.normed_t[...], kv_low[:, HD:]).astype(BF)
    for copy in more:
        copy.wait()
    heads = extra[0:1, :].astype(F32)
    for d in range(3):
        heads = heads + xgot[d, 0:1, :].astype(F32)
    hg[4:5, :] = heads
    hg[5:6, :] = jnp.sum(acc[3, :, :HD], axis=0, keepdims=True)
    second.finish()

    @pl.loop(0, 16)
    def _(b):
        at = pl.ds(pl.multiple_of(b * 16, 16), 16)
        dn = total2[at, :].astype(F32) + dn_kv[at, :]
        dv, dg = norm_back(i.tokens[at, :].astype(F32), i.gains[0:1, :], dn)
        acc[0] += dg
        o.grad_tokens[at, :] = d_mid[at, :] + dv

    for g in range(3):
        gt[g : g + 1, :] = jnp.sum(acc[g], axis=0, keepdims=True)
    gt[3:4, :] = i.dg3[...]
    last = gt[...].T
    heads_t = hg[...].T
    tail[:, 2 * HD :] = last.astype(BF)
    for f in range(4):
        tail[288 * f : 288 * f + 64, 2 * HD :] = (
            last[288 * f : 288 * f + 64] + heads_t[64 * f : 64 * f + 64]
        ).astype(BF)
    rkv.one()
    up.four()
    gate.fourb()
    rkv.two()
    roq.three()
    down.fiveb()
    up.fourb()
    rkv.three()
    roq.four()
    gate.five()
    rkv.four()
    rkv.fourb()
    roq.fourb()
    up.five()
    gate.fiveb()
    down.six()
    rkv.five()
    rkv.fiveb()
    roq.five()
    up.fiveb()
    gate.six()
    roq.fiveb()
    rkv.six()
    roq.six()
    up.six()
    for d in range(8):
        for e in (1, 2, 3):
            key_copy(p.c, d, e).wait_send()
    for d in range(1, 8):
        value_copy(p.c, d).wait_send()
    for copy in kv2 + keys_far + values_far + gate.c1 + up.c1 + roq.c1 + rkv.c1:
        copy.wait_send()


def zsum_buffers(share):
    return [pltpu.VMEM((3, share, 1152), BF)] + sems(3) + sems(3)


def back_call(ins, cid):
    scratch = (
        [pltpu.VMEM((256, 1152), BF)]
        + zsum_buffers(32) * 2
        + [pltpu.VMEM((256, 1152), BF)]
        + zsum_buffers(64)
        + [
            pltpu.VMEM((16, HD), BF),
            pltpu.VMEM((3, 16, HD), BF),
            pltpu.VMEM((256, 1152), F32),
            pltpu.VMEM((256, 1152), BF),
            pltpu.VMEM((256, HD), BF),
            pltpu.VMEM((256, 1), F32),
            pltpu.VMEM((256, HD), F32),
            pltpu.VMEM((8, 256, 2 * HD), BF),
            pltpu.VMEM((3, 8, 64, HD), BF),
            pltpu.VMEM((7, 256, HD), BF),
            pltpu.VMEM((8, 64, HD), BF),
            pltpu.VMEM((256, HD), BF),
            pltpu.VMEM((7, 64, HD), BF),
            pltpu.VMEM((3, 64, HD), BF),
            pltpu.VMEM((256, 2 * HD), BF),
            pltpu.VMEM((256, 1152), F32),
            pltpu.VMEM((4, 16, 1152), F32),
            pltpu.VMEM((128, 1152), F32),
            pltpu.VMEM((128, HD), F32),
            pltpu.VMEM((1152, 512), BF),
            pltpu.VMEM((1152, 640), BF),
        ]
        + sems(24)
        + sems(7)
        + sems(7)
        + sems(3)
        + sems(3)
        + sems(3)
        + reduce_buffers(1728, 896, True) * 2
        + reduce_buffers(1728, 896, False)
        + reduce_buffers(512, 256, False)
        + reduce_buffers(640, 384, False)
    )
    shapes = [((256, 1152), F32)] + [((288, n), BF) for n in (1728, 1728, 1728, 256, 256, 256, 256, 128)]
    return pl.pallas_call(
        back_kernel,
        out_shape=[jax.ShapeDtypeStruct(*shape) for shape in shapes],
        in_specs=[VM] * len(ins),
        out_specs=[VM] * len(shapes),
        scratch_shapes=scratch,
        compiler_params=params(cid, 62),
        name="backward",
    )(*ins)


class ForeIn(NamedTuple):
    tokens: Any
    cot: Any
    w_query: Any
    w_key: Any
    w_value: Any
    w_out: Any
    columns: Any
    w_gate: Any
    w_up: Any
    w_down: Any
    cosine: Any
    sine: Any
    key_pos: Any
    query_pos: Any

class ForeOut(NamedTuple):
    out: Any
    small: Any
    gains: Any
    heads: Any
    x: Any
    d_ffn_t: Any
    hidden: Any
    normed2_t: Any
    d_gate: Any
    d_up: Any
    middle: Any
    branch: Any
    dg3: Any
    attn: Any
    attn_low: Any
    lse: Any
    queries: Any
    kv: Any
    normed_t: Any
    q_proj: Any
    k_proj: Any

TILES = [(c0, min(c0 + 256, 1728)) for c0 in range(0, 1728, 256)]


def turn(v, cosine, sine):
    v1, v2 = v[:, :128], v[:, 128:]
    return jnp.concatenate([v1 * cosine - v2 * sine, v2 * cosine + v1 * sine], axis=1)


def transpose_into(dst, src):
    for c0 in range(0, 1152, 128):
        dst[c0 : c0 + 128, :] = src[:, c0 : c0 + 128].astype(F32).T.astype(BF)


def fore_kernel(*refs):
    n_in, n_out = len(ForeIn._fields), len(ForeOut._fields)
    i = ForeIn(*refs[:n_in])
    o = ForeOut(*refs[n_in : n_in + n_out])
    rest = list(refs[n_in + n_out :])

    def take(n):
        got = rest[:n]
        del rest[:n]
        return got

    p = Place()
    scale = HD ** (-0.5)
    w_gate, w_up, w_down, act, slope, normed, d_ffn, probs, head_cols, accg = take(10)
    local, gs, gr, ks, kr, vs, vr, fs, fr = take(9)
    total1, total2 = take(2)
    z1, z2 = take(10), take(10)
    part, pack = take(2)
    small = o.small
    halves = [(h, slice(128 * h, 128 * h + 128)) for h in (0, 1)]
    firsts = [ZSum(p, part, total1, 128 * h, *z1[5 * h : 5 * h + 5]) for h in (0, 1)]
    seconds = [ZSum(p, part, total2, 128 * h, *z2[5 * h : 5 * h + 5]) for h in (0, 1)]
    kv = o.kv
    gathers = [
        Gather(p, src, dst, local.at[j], gs, gr, 6 * j, j > 0)
        for j, (src, dst) in enumerate(
            [(pack, small), (i.w_gate, w_gate), (i.w_up, w_up), (i.w_down, w_down)]
        )
    ]
    g_small, g_gate, g_up, g_down = gathers

    greet([p.sib(), p.dy(1), p.dy(3)] + [p.dc(d) for d in range(1, 8)] + [p.dz(d) for d in (1, 2, 3)])
    for ref, c0 in ((i.w_query, 0), (i.w_key, 256), (i.w_value, 512), (i.w_out, 768)):
        pack[:, c0 : c0 + 256] = ref[...]
    pack[:, 1024:] = i.columns[...]
    g_small.start()
    g_small.start_far()
    g_gate.start()
    g_up.start()
    g_down.start()
    accg[...] = jnp.zeros_like(accg)
    g_small.forward()
    g_gate.start_far()
    g_small.finish()

    o.gains[...] = small[:, 1024:].astype(F32).T[:8, :]
    for f in range(4):
        head_cols[64 * f : 64 * f + 64, :] = small[288 * f : 288 * f + 64, 1024:].astype(F32)
    o.heads[...] = head_cols[...].T[:8, :]

    @pl.loop(0, 16)
    def _(b):
        at = pl.ds(pl.multiple_of(b * 16, 16), 16)
        normed[at, :] = normalize(i.tokens[at, :].astype(F32), o.gains[0:1, :]).astype(BF)

    o.q_proj[...] = plain(normed[...], small[:, :256])
    o.k_proj[...] = plain(normed[...], small[:, 256:512])
    kv[p.c, :, HD:] = plain(normed[...], small[:, 512:768]).astype(BF)

    quarter = pl.ds(pl.multiple_of(p.z * 64, 64), 64)
    sent = [
        send(
            kv.at[p.c, quarter, pl.ds(HD, HD)],
            kv.at[p.c, quarter, pl.ds(HD, HD)],
            vs.at[d - 1],
            vr.at[d - 1],
            p.dc(d),
        )
        for d in range(1, 8)
    ]

    @pl.loop(0, 4)
    def _(b):
        at = pl.ds(pl.multiple_of(b * 64, 64), 64)
        n = normalize(o.k_proj[at, :], o.heads[5:6, :])
        kv[p.c, at, :HD] = turn(n, i.cosine[at, :], i.sine[at, :]).astype(BF)

    keys = kv.at[p.c, :, pl.ds(0, HD)]
    sent_k = [send(keys, keys, ks.at[d - 1], kr.at[d - 1], p.dc(d)) for d in range(1, 8)]

    @pl.loop(0, 4)
    def _(b):
        at = pl.ds(pl.multiple_of(b * 64, 64), 64)
        n = normalize(o.q_proj[at, :], o.heads[4:5, :])
        o.queries[at, :] = turn(n, i.cosine[at, :], i.sine[at, :]).astype(BF)

    g_gate.across()
    g_up.start_far()
    for copy in sent:
        copy.wait_recv()
    sent_z = []
    for d in range(8):
        block = kv.at[(p.c + 8 - d) % 8, quarter, pl.ds(HD, HD)]
        if d == 0:
            continue
        sent_z += [
            send(block, block, fs.at[3 * d + e - 1], fr.at[3 * d + e - 1], p.dz(e))
            for e in (2, 1, 3)
        ]
    transpose_into(o.normed_t, normed)
    for copy in sent_k:
        copy.wait_recv()
    g_gate.forward()
    g_down.start_far()

    @pl.loop(0, 4)
    def _(b):
        at = pl.ds(pl.multiple_of(b * 64, 64), 64)
        query = o.queries[at, :]
        seen = [i.key_pos[kb] <= i.query_pos[at, :] for kb in range(8)]
        scores = [against(query, kv[kb, :, :HD]) * scale for kb in range(8)]
        top = jnp.max(jnp.where(seen[0], scores[0], -1e30), axis=-1, keepdims=True)
        for kb in range(1, 8):
            top = jnp.maximum(
                top, jnp.max(jnp.where(seen[kb], scores[kb], -1e30), axis=-1, keepdims=True)
            )
        scores = [jnp.where(seen[kb], jnp.exp(scores[kb] - top), 0.0) for kb in range(8)]
        total = jnp.sum(scores[0], axis=-1, keepdims=True)
        for kb in range(1, 8):
            total = total + jnp.sum(scores[kb], axis=-1, keepdims=True)
        o.lse[at, :] = top + jnp.log(total)
        share = 1.0 / total
        for kb in range(8):
            probs[kb, at, :] = (scores[kb] * share).astype(BF)

    g_up.across()
    for copy in sent_z:
        copy.wait_recv()
    attn = plain(probs[0], kv[0, :, HD:])
    for kb in range(1, 8):
        attn = attn + plain(probs[kb], kv[kb, :, HD:])
    o.attn[...] = attn
    attn_low = attn.astype(BF)
    o.attn_low[...] = attn_low
    for h, rows in halves:
        part[rows, :] = against(attn_low[rows], small[:, 768:1024]).astype(BF)
        firsts[h].start()
    g_up.forward()
    g_down.across()
    for half in firsts:
        half.middle()
    g_gate.finish()

    def middle_rows(b):
        at = pl.ds(pl.multiple_of(b * 16, 16), 16)
        branch = total1[at, :]
        o.branch[at, :] = branch
        middle = i.tokens[at, :].astype(F32) + normalize(
            branch.astype(F32), o.gains[1:2, :]
        )
        o.middle[at, :] = middle
        normed[at, :] = normalize(middle, o.gains[2:3, :]).astype(BF)

    for h, rows in halves:
        firsts[h].finish()
        pl.loop(8 * h, 8 * h + 8)(middle_rows)
    g_up.finish()
    for c0, c1 in TILES:
        gate = plain(normed[...], w_gate[:, c0:c1])
        up = plain(normed[...], w_up[:, c0:c1])
        bend = jnp.tanh(0.7978845608028654 * (gate + 0.044715 * gate * gate * gate))
        gelu = 0.5 * gate * (1.0 + bend)
        o.hidden[:, c0:c1] = (gelu * up).astype(BF)
        act[:, c0:c1] = gelu
        rise = 0.7978845608028654 * (1.0 + 0.134145 * gate * gate)
        slope[:, c0:c1] = up * (0.5 * (1.0 + bend) + 0.5 * gate * (1.0 - bend * bend) * rise)
    g_down.forward()
    g_down.finish()
    for h, rows in halves:
        for c0 in range(0, 1152, 384):
            part[rows, c0 : c0 + 384] = against(
                o.hidden[rows, :], w_down[c0 : c0 + 384, :]
            ).astype(BF)
        seconds[h].start()
    transpose_into(o.normed2_t, normed)
    for half in seconds:
        half.middle()

    def last_rows(b):
        at = pl.ds(pl.multiple_of(b * 16, 16), 16)
        ffn = total2[at, :].astype(F32)
        o.out[at, :] = (o.middle[at, :] + normalize(ffn, o.gains[3:4, :])).astype(BF)
        dv, dg = norm_back(ffn, o.gains[3:4, :], i.cot[at, :].astype(F32))
        accg[...] += dg
        d_ffn[at, :] = dv.astype(BF)

    for h, rows in halves:
        seconds[h].finish()
        pl.loop(8 * h, 8 * h + 8)(last_rows)
    o.dg3[...] = jnp.sum(accg[...], axis=0, keepdims=True)
    transpose_into(o.d_ffn_t, d_ffn)
    for c0, c1 in TILES:
        d_hidden = plain(d_ffn[...], w_down[:, c0:c1])
        o.d_up[:, c0:c1] = (d_hidden * act[:, c0:c1]).astype(BF)
        o.d_gate[:, c0:c1] = (d_hidden * slope[:, c0:c1]).astype(BF)
    for c0 in range(0, 1152, 384):
        o.x[:, c0 : c0 + 384] = (
            against(o.d_gate[...], w_gate[c0 : c0 + 384, :])
            + against(o.d_up[...], w_up[c0 : c0 + 384, :])
        ).astype(BF)
    for copy in sent + sent_k + sent_z:
        copy.wait_send()


def fore_call(ins, cid):
    scratch = (
        [pltpu.VMEM((1152, 1728), BF)] * 3
        + [
            pltpu.VMEM((256, 1728), F32),
            pltpu.VMEM((256, 1728), F32),
            pltpu.VMEM((256, 1152), BF),
            pltpu.VMEM((256, 1152), BF),
            pltpu.VMEM((8, 256, 256), BF),
            pltpu.VMEM((256, 128), F32),
            pltpu.VMEM((16, 1152), F32),
            pltpu.SemaphoreType.DMA((4,)),
        ]
        + sems(24)
        + sems(7)
        + sems(7)
        + sems(24)
        + [pltpu.VMEM((256, 1152), BF)] * 2
        + zsum_buffers(32) * 4
        + [pltpu.VMEM((256, 1152), BF), pltpu.VMEM((288, 1152), BF)]
    )
    shapes = ForeOut(
        out=((256, 1152), BF),
        small=((1152, 1152), BF),
        gains=((8, 1152), F32),
        heads=((8, 256), F32),
        x=((256, 1152), BF),
        d_ffn_t=((1152, 256), BF),
        hidden=((256, 1728), BF),
        normed2_t=((1152, 256), BF),
        d_gate=((256, 1728), BF),
        d_up=((256, 1728), BF),
        middle=((256, 1152), F32),
        branch=((256, 1152), BF),
        dg3=((1, 1152), F32),
        attn=((256, 256), F32),
        attn_low=((256, 256), BF),
        lse=((256, 1), F32),
        queries=((256, 256), BF),
        kv=((8, 256, 512), BF),
        normed_t=((1152, 256), BF),
        q_proj=((256, 256), F32),
        k_proj=((256, 256), F32),
    )
    done = pl.pallas_call(
        fore_kernel,
        out_shape=[jax.ShapeDtypeStruct(*shape) for shape in shapes],
        in_specs=[VM] * len(ins),
        out_specs=[VM] * len(shapes),
        scratch_shapes=scratch,
        compiler_params=params(cid, 62),
        name="forward",
    )(*ins)
    return ForeOut(*done)


def final_kernel(*refs):
    ins, outs = refs[:10], refs[10:21]
    held, wide, (rows_ref, heads_ref, s_in, s_out) = refs[21:31], refs[31:38], refs[38:]
    loads = [pltpu.make_async_copy(ins[n], held[n], s_in.at[n]) for n in range(10)]
    for copy in loads:
        copy.start()
    stores = []
    for n in range(9):
        loads[n].wait()
        if n > 1:
            wide[n - 2][...] = held[n][...].astype(F32)
        copy = pltpu.make_async_copy(held[n] if n < 2 else wide[n - 2], outs[n], s_out.at[n])
        copy.start()
        stores.append(copy)
    loads[9].wait()
    columns = held[9][...].astype(F32).T
    rows_ref[...] = columns[:4, :]
    heads_ref[...] = columns[4:6, :64]
    for n, ref in ((9, rows_ref), (10, heads_ref)):
        copy = pltpu.make_async_copy(ref, outs[n], s_out.at[n])
        copy.start()
        stores.append(copy)
    for copy in stores:
        copy.wait()


def final_call(*ins):
    grads = [a.shape for a in ins[2:9]]
    shapes = [ins[0].shape, ins[1].shape] + grads + [(4, 288), (2, 64)]
    any_space = pl.BlockSpec(memory_space=pl.ANY)
    return pl.pallas_call(
        final_kernel,
        out_shape=[
            jax.ShapeDtypeStruct(shape, BF if n == 0 else F32) for n, shape in enumerate(shapes)
        ],
        in_specs=[any_space] * 10,
        out_specs=[any_space] * 11,
        scratch_shapes=[pltpu.VMEM(a.shape, a.dtype) for a in ins]
        + [pltpu.VMEM(shape, F32) for shape in grads]
        + [
            pltpu.VMEM((4, 288), F32),
            pltpu.VMEM((2, 64), F32),
            pltpu.SemaphoreType.DMA((10,)),
            pltpu.SemaphoreType.DMA((11,)),
        ],
        compiler_params=pltpu.CompilerParams(vmem_limit_bytes=62 * 2**20),
        name="final",
    )(*ins)


def per_device(
    tokens,
    block_order,
    cotangent,
    w_query,
    w_key,
    w_value,
    w_out,
    w_gate,
    w_up,
    w_down,
    gains,
    head_gains,
):
    _, rows, width = tokens.shape
    cycle_index = lax.axis_index("context")
    span = rows // 2
    seq_len = rows * 8

    columns = jnp.pad(
        jnp.concatenate([gains.T, jnp.pad(head_gains.T, ((0, 288 - 64), (0, 0)))], axis=1),
        ((0, 0), (0, 122)),
    )
    offsets = jnp.arange(seq_len, dtype=jnp.int32)
    key_pos = (jnp.repeat(block_order, span, axis=1) * span + (offsets % span)[None, :])[0]
    query_pos = lax.dynamic_slice_in_dim(key_pos, cycle_index * rows, rows, 0)
    cosine, sine = tables(query_pos)
    ins = ForeIn(
        tokens=tokens[0],
        cot=cotangent[0],
        w_query=w_query,
        w_key=w_key,
        w_value=w_value,
        w_out=w_out.T,
        columns=columns,
        w_gate=w_gate,
        w_up=w_up,
        w_down=w_down.T,
        cosine=cosine,
        sine=sine,
        key_pos=key_pos.reshape(8, 1, rows),
        query_pos=query_pos[:, None],
    )
    held = fore_call(ins, 1)
    grad_tokens, sum_down, sum_gate, sum_up, sum_q, sum_o, sum_k, sum_v, last = back_call(
        BackIn(
            x=held.x,
            d_ffn_t=held.d_ffn_t,
            hidden=held.hidden,
            normed2_t=held.normed2_t,
            d_gate=held.d_gate,
            d_up=held.d_up,
            middle=held.middle,
            branch=held.branch,
            cot=ins.cot,
            tokens=ins.tokens,
            gains=held.gains,
            dg3=held.dg3,
            attn=held.attn,
            attn_low=held.attn_low,
            lse=held.lse,
            queries=held.queries,
            kv=held.kv,
            key_pos=ins.key_pos,
            query_pos=ins.query_pos,
            small=held.small,
            normed_t=held.normed_t,
            q_proj=held.q_proj,
            k_proj=held.k_proj,
            heads=held.heads,
            cosine=ins.cosine,
            sine=ins.sine,
        ),
        2,
    )
    done = final_call(
        held.out, grad_tokens, sum_gate, sum_up, sum_down, sum_q, sum_k, sum_v, sum_o, last
    )
    result, d_tokens, d_gate, d_up, d_down, d_q, d_k, d_v, d_o, d_gains, d_heads = done
    return (
        result[None],
        d_tokens[None],
        d_q,
        d_k,
        d_v,
        d_o.T,
        d_gate,
        d_up,
        d_down.T,
        d_gains,
        d_heads,
    )


def solution(mesh):
    in_specs = (
        P("fsdp", "context", None),
        P("fsdp", None),
        P("fsdp", "context", None),
        P("fsdp", "tensor"),
        P("fsdp", None),
        P("fsdp", None),
        P("tensor", "fsdp"),
        P("fsdp", "tensor"),
        P("fsdp", "tensor"),
        P("tensor", "fsdp"),
        P(None, "fsdp"),
        P(None, "fsdp"),
    )
    out_specs = (
        P("fsdp", "context", None),
        P("fsdp", "context", None),
        P("fsdp", "tensor"),
        P("fsdp", None),
        P("fsdp", None),
        P("tensor", "fsdp"),
        P("fsdp", "tensor"),
        P("fsdp", "tensor"),
        P("tensor", "fsdp"),
        P(None, "fsdp"),
        P(None, "fsdp"),
    )
    return jax.shard_map(
        per_device, mesh=mesh, in_specs=in_specs, out_specs=out_specs, check_vma=False
    )
```

```python
import functools
import math
from typing import Any, NamedTuple

import jax
import jax.numpy as jnp
from jax import lax
from jax.experimental import pallas as pl
from jax.experimental.pallas import tpu as pltpu
from jax.sharding import PartitionSpec as P

HD = 256
ROPE_BASE = 1000000.0
EPS = 1e-06
MESH = pl.DeviceIdType.MESH
BF = jnp.bfloat16
F32 = jnp.float32


def normalize(values, gain):
    return values * lax.rsqrt(jnp.mean(values * values, axis=-1, keepdims=True) + EPS) * gain


def rotate(values, cosine, sine):
    middle = values.shape[-1] // 2
    first = values[..., :middle]
    second = values[..., middle:]
    return jnp.concatenate(
        [first * cosine - second * sine, second * cosine + first * sine], axis=-1
    )


def tables(positions):
    steps = jnp.arange(HD // 2, dtype=jnp.float32) * (2.0 / HD)
    inverse = jnp.exp(-math.log(ROPE_BASE) * steps)
    angle = positions.astype(jnp.float32)[:, None] * inverse[None, :]
    return (jnp.cos(angle), jnp.sin(angle))


def plain(left, right):
    return jnp.dot(left, right, preferred_element_type=jnp.float32)


def inner(left, right):
    return lax.dot_general(
        left, right, (((0,), (0,)), ((), ())), preferred_element_type=jnp.float32
    )


def against(left, right):
    return lax.dot_general(
        left, right, (((1,), (1,)), ((), ())), preferred_element_type=jnp.float32
    )


class Place:
    def __init__(self):
        f = lax.axis_index("fsdp")
        c = lax.axis_index("context")
        self.f, self.c, self.z = f, c, lax.axis_index("tensor")
        self.ylo, self.core = f // 2, f % 2
        self.x, self.yhi = c // 2, c % 2
        self.y = self.yhi * 2 + self.ylo

    def at(self, x=None, y=None, z=None, core=None):
        x = self.x if x is None else x
        y = self.y if y is None else y
        z = self.z if z is None else z
        core = self.core if core is None else core
        return ((y % 2) * 2 + core, x * 2 + y // 2, z)

    def sib(self):
        return self.at(core=1 - self.core)

    def dy(self, d):
        return self.at(y=(self.y + d) % 4)

    def dx(self, d):
        return self.at(x=(self.x + d) % 4)

    def dz(self, d):
        return self.at(z=(self.z + d) % 4)

    def dc(self, d):
        return (self.f, (self.c + d) % 8, self.z)


def greet(devices):
    barrier = pltpu.get_barrier_semaphore()
    for device in devices:
        pl.semaphore_signal(barrier, inc=1, device_id=device, device_id_type=MESH)
    pl.semaphore_wait(barrier, len(devices))


def send(src, dst, ssem, rsem, device):
    copy = pltpu.make_async_remote_copy(
        src_ref=src, dst_ref=dst, send_sem=ssem, recv_sem=rsem, device_id=device, device_id_type=MESH
    )
    copy.start()
    return copy


def sems(n):
    return [pltpu.SemaphoreType.DMA((n,)), pltpu.SemaphoreType.DMA((n,))]


VM = pl.BlockSpec(memory_space=pltpu.VMEM)
HB = pl.BlockSpec(memory_space=pl.ANY)


def params(cid, limit=48):
    return pltpu.CompilerParams(
        collective_id=cid, has_side_effects=True, vmem_limit_bytes=limit * 2**20
    )


class Gather:
    def __init__(self, place, src, out, local, ssem, rsem, base, relay=False):
        self.p, self.src, self.out = place, src, out
        self.local, self.ssem, self.rsem, self.base = local, ssem, rsem, base
        self.rows, self.relay = src.shape[0], relay

    def go(self, n, src, dst, device):
        return send(src, dst, self.ssem.at[self.base + n], self.rsem.at[self.base + n], device)

    def at(self, row, n):
        return self.out.at[pl.ds(pl.multiple_of(row, 16), n)]

    def start(self):
        p, rows = self.p, self.rows
        own = self.at(p.f * rows, rows)
        self.s = self.go(2, self.src, own, p.sib())
        self.l = pltpu.make_async_copy(self.src, own, self.local)
        self.l.start()

    def start_far(self):
        p, rows, half = self.p, self.rows, self.rows // 2
        first, n = (64 * (p.x % 2), 80) if self.relay else (0, half)
        self.y = []
        for h, d in ((0, 1), (1, 3)):
            row = first + half * h
            src = self.src.at[pl.ds(pl.multiple_of(row, 16), n)]
            self.y.append(self.go(h, src, self.at(p.f * rows + row, n), p.dy(d)))

    def across(self):
        p, half = self.p, self.rows // 2
        for copy in self.y:
            copy.wait_recv()
        row = (2 * (1 - p.ylo) + p.core) * self.rows
        flip, back = p.x + 1 - 2 * (p.x % 2), 3 - p.x
        self.w = []
        for h, x in ((0, flip), (1, back)):
            part = self.at(row + half * h + 80 * (p.x % 2), 64)
            self.w.append(self.go(4 + h, part, part, p.at(x=x)))

    def forward(self):
        p, rows = self.p, self.rows
        for copy in self.w if self.relay else self.y:
            copy.wait_recv()
        block = self.at((2 * (1 - p.ylo) + p.core) * rows, rows)
        self.t = self.go(3, block, block, p.sib())

    def finish(self):
        self.l.wait()
        for copy in self.y:
            copy.wait_send()
        if self.relay:
            for copy in self.w:
                copy.wait_send()
        self.s.wait()
        self.t.wait()


class ZSum:
    def __init__(self, place, x, out, base, got, s1, r1, s2, r2):
        self.p, self.x, self.got, self.out = place, x, got, out
        self.base, self.share = base, got.shape[1]
        self.s1, self.r1, self.s2, self.r2 = s1, r1, s2, r2

    def rows(self, block):
        return pl.ds(pl.multiple_of(self.base + block * self.share, 32), self.share)

    def start(self):
        p = self.p
        self.c1 = [
            send(
                self.x.at[self.rows((p.z + d) % 4)],
                self.got.at[d - 1],
                self.s1.at[d - 1],
                self.r1.at[d - 1],
                p.dz(d),
            )
            for d in (2, 1, 3)
        ]

    def middle(self):
        p = self.p
        for copy in self.c1:
            copy.wait_recv()
        own = self.rows(p.z)

        @pl.loop(0, self.share // 16)
        def _(i):
            at = pl.ds(pl.multiple_of(self.base + p.z * self.share + i * 16, 16), 16)
            to = pl.ds(pl.multiple_of(i * 16, 16), 16)
            total = self.x[at, :].astype(F32)
            for d in range(3):
                total = total + self.got[d, to, :].astype(F32)
            self.out[at, :] = total.astype(BF)

        self.c2 = [
            send(self.out.at[own], self.out.at[own], self.s2.at[d - 1], self.r2.at[d - 1], p.dz(d))
            for d in (2, 1, 3)
        ]

    def finish(self):
        for copy in self.c1:
            copy.wait_send()
        for copy in self.c2:
            copy.wait()


class Reduce:
    def __init__(self, place, out, bufs, cut, src=None, left=None, right=None, direct=False):
        self.p, self.src, self.left, self.right = place, src, left, right
        self.outs, self.cut = out, cut
        if src is None:
            self.sent, bufs = bufs[0], bufs[1:]
        self.r1, self.r2, self.q, self.r3, self.r4, self.r5, self.r6, self.s, self.r = bufs
        self.n = sum(ref.shape[1] for ref in out)
        self.ns, self.direct = 0, direct
        x, side = place.x, (cut // 128 + 1) // 2 * 128
        flip, back = x + 1 - 2 * (x % 2), 3 - x
        self.ways = [
            (flip, back, 3 - flip, pl.ds(0, side)),
            (back, flip, back + 1 - 2 * (back % 2), pl.ds(side, cut - side)),
        ]

    def go(self, src, dst, device):
        i = self.ns
        self.ns += 1
        return send(src, dst, self.s.at[i], self.r.at[i], device)

    def rows(self, block):
        return pl.ds(pl.multiple_of(block * 288, 16), 288)

    def product(self, block, c0, c1):
        return plain(self.left[self.rows(block), :], self.right[:, c0:c1])

    def tiles(self):
        return [(c0, min(c0 + 256, self.n)) for c0 in range(0, self.n, 256)]

    def one(self):
        p = self.p
        if self.src is None:

            @pl.loop(0, 2)
            def _(j):
                for c0, c1 in self.tiles():
                    self.sent[j, :, c0:c1] = self.product(2 * j + 1 - p.core, c0, c1).astype(BF)

            blocks = [self.sent.at[j] for j in (0, 1)]
        else:
            blocks = [self.src.at[self.rows(2 * j + 1 - p.core)] for j in (0, 1)]
        self.c1 = [self.go(blocks[j], self.r1.at[j], p.sib()) for j in (0, 1)]

    def two(self):
        p = self.p
        for copy in self.c1:
            copy.wait_recv()
        if self.src is None:

            @pl.loop(0, 2)
            def _(j):
                for c0, c1 in self.tiles():
                    self.r1[j, :, c0:c1] = (
                        self.product(2 * j + p.core, c0, c1) + self.r1[j, :, c0:c1].astype(F32)
                    ).astype(BF)

        else:

            @pl.loop(0, 18)
            def _(i):
                at = pl.ds(pl.multiple_of(i * 16, 16), 16)
                for j in (0, 1):
                    row = pl.multiple_of((2 * j + p.core) * 288 + i * 16, 16)
                    own = self.src[pl.ds(row, 16), :]
                    self.r1[j, at, :] = (own.astype(F32) + self.r1[j, at, :].astype(F32)).astype(BF)

        far = 1 - p.ylo
        self.c2 = [
            self.go(self.r1.at[far, pl.ds(0, 144)], self.r2.at[pl.ds(0, 144)], p.dy(1)),
            self.go(self.r1.at[far, pl.ds(144, 144)], self.r2.at[pl.ds(144, 144)], p.dy(3)),
        ]

    def three(self):
        p, cut = self.p, self.cut
        for copy in self.c2:
            copy.wait_recv()
        rest = self.n - cut

        @pl.loop(0, 9)
        def _(i):
            for h in (0, 1):
                at = pl.ds(pl.multiple_of(h * 144 + i * 16, 16), 16)
                to = pl.ds(pl.multiple_of(i * 16, 16), 16)
                total = (self.r1[p.ylo, at, :].astype(F32) + self.r2[at, :].astype(F32)).astype(BF)
                self.q[2 * h, to, :] = total[:, :cut]
                if rest == cut:
                    self.q[2 * h + 1, to, :] = total[:, cut:]
                else:
                    self.q[2 * h + 1, to, :] = jnp.concatenate(
                        [total[:, cut:], jnp.zeros((16, cut - rest), BF)], axis=1
                    )

        if self.direct:
            self.c3 = [
                self.go(self.q.at[(p.x + d) % 4], self.r3.at[d - 1], p.dx(d)) for d in (2, 1, 3)
            ]
            return
        self.c3 = []
        for one, two, theirs, cols in self.ways:
            for k, quarter in enumerate((one, theirs)):
                self.c3.append(
                    self.go(self.q.at[quarter, :, cols], self.r3.at[k, :, cols], p.at(x=one))
                )

    def sum_rows(self, dst, first, *more):
        @pl.loop(0, 9)
        def _(i):
            at = pl.ds(pl.multiple_of(i * 16, 16), 16)
            total = first[at, :].astype(F32)
            for ref in more:
                total = total + ref[at, :].astype(F32)
            dst[at, :] = total.astype(BF)

    def four(self):
        p = self.p
        for copy in self.c3:
            copy.wait_recv()
        if self.direct:
            return
        mine = self.q.at[p.x]
        self.sum_rows(mine, mine, self.r3.at[0])
        self.c3b = []
        for one, two, _, cols in self.ways:
            held = self.q.at[two, :, cols]
            self.sum_rows(held, held, self.r3.at[1, :, cols])
            self.c3b.append(self.go(held, self.r3.at[2, :, cols], p.at(x=two)))

    def fourb(self):
        p = self.p
        if self.direct:
            self.sum_rows(self.r6, self.q.at[p.x], *[self.r3.at[d] for d in range(3)])
        else:
            for copy in self.c3b:
                copy.wait_recv()
            self.sum_rows(self.r6, self.q.at[p.x], self.r3.at[2])
        self.c4 = self.go(self.r6, self.r4, p.dy(2))

    def five(self):
        p = self.p
        self.c4.wait()
        mine = self.r5.at[p.x]
        self.sum_rows(mine, self.r6, self.r4)
        if self.direct:
            self.c5 = [self.go(mine, mine, p.dx(d)) for d in (2, 1, 3)]
            return
        self.c5 = []
        for one, two, _, cols in self.ways:
            part = self.r5.at[p.x, :, cols]
            self.c5.append(self.go(part, part, p.at(x=two)))
            self.c5.append(self.go(part, part, p.at(x=one)))

    def fiveb(self):
        p = self.p
        self.c5b = []
        if self.direct:
            return
        for k, (one, two, _, cols) in enumerate(self.ways):
            self.c5[2 * k].wait_recv()
            part = self.r5.at[two, :, cols]
            self.c5b.append(self.go(part, part, p.at(x=one)))

    def put(self, rows, c0, value):
        start = 0
        for ref in self.outs:
            end = start + ref.shape[1]
            lo, hi = max(c0, start), min(c0 + value.shape[1], end)
            if lo < hi:
                ref[rows, lo - start : hi - start] = value[:, lo - c0 : hi - c0]
            start = end

    def six(self):
        rest = self.n - self.cut
        for copy in self.c5b + (self.c5 if self.direct else self.c5[1::2]):
            copy.wait_recv()

        @pl.loop(0, 9)
        def _(i):
            at = pl.ds(pl.multiple_of(i * 16, 16), 16)
            for h in (0, 1):
                to = pl.ds(pl.multiple_of(h * 144 + i * 16, 16), 16)
                self.put(to, 0, self.r5[2 * h, at, :])
                self.put(to, self.cut, self.r5[2 * h + 1, at, :rest])

        for copy in self.c2 + self.c3 + self.c5 + self.c5b:
            copy.wait_send()
        if not self.direct:
            for copy in self.c3b:
                copy.wait_send()


def reduce_buffers(n, cut, computed):
    bufs = [
        pltpu.VMEM((2, 288, n), BF),
        pltpu.VMEM((288, n), BF),
        pltpu.VMEM((4, 144, cut), BF),
        pltpu.VMEM((3, 144, cut), BF),
        pltpu.VMEM((144, cut), BF),
        pltpu.VMEM((4, 144, cut), BF),
        pltpu.VMEM((144, cut), BF),
    ] + sems(20)
    return [pltpu.VMEM((2, 288, n), BF)] + bufs if computed else bufs


def norm_back(v, gain, dy):
    r = lax.rsqrt(jnp.mean(v * v, axis=-1, keepdims=True) + EPS)
    gdy = gain * dy
    dv = r * gdy - v * (r * r * r * jnp.mean(gdy * v, axis=-1, keepdims=True))
    return dv, r * v * dy


def turn_back(d, cosine, sine):
    d1, d2 = d[:, :128], d[:, 128:]
    return jnp.concatenate([d1 * cosine + d2 * sine, d2 * cosine - d1 * sine], axis=1)


class BackIn(NamedTuple):
    x: Any
    d_ffn_t: Any
    hidden: Any
    normed2_t: Any
    d_gate: Any
    d_up: Any
    middle: Any
    branch: Any
    cot: Any
    tokens: Any
    gains: Any
    dg3: Any
    attn: Any
    attn_low: Any
    lse: Any
    queries: Any
    kv: Any
    key_pos: Any
    small: Any
    normed_t: Any
    q_proj: Any
    k_proj: Any
    heads: Any
    cosine: Any
    sine: Any

class BackOut(NamedTuple):
    grad_tokens: Any
    o_down: Any
    o_gate: Any
    o_up: Any
    o_q: Any
    o_o: Any
    o_k: Any
    o_v: Any
    o_last: Any


def back_kernel(*refs):
    n_in, n_out = len(BackIn._fields), len(BackOut._fields)
    o = BackOut(*refs[n_in : n_in + n_out])
    rest = list(refs[n_in + n_out :])

    def take(n):
        got = rest[:n]
        del rest[:n]
        return got

    i = BackIn(*take(n_in))
    loading = take(1)[0]
    loads = BackIn(
        *[pltpu.make_async_copy(refs[n], i[n], loading.at[n]) for n in range(n_in)]
    )
    for copy in loads:
        copy.start()
    p = Place()
    scale = HD ** (-0.5)
    total1 = take(1)[0]
    own_pos = take(1)[0]
    z1 = take(10)
    total2 = take(1)[0]
    z2 = take(5)
    (extra, xgot, d_mid, d_branch, d_attn, delta, dq, parts) = take(8)
    got_k, got_v, k_sum, v_sum, far_k, far_v = take(6)
    (kv_low, dn_kv, acc, gt, hg, oq, tail) = take(7)
    ks, kr, vs, vr, ks2, kr2, vs2, vr2, os, orr, xs, xr = take(12)
    down = Reduce(p, [o.o_down], take(10), 896, left=i.d_ffn_t, right=i.hidden)
    gate = Reduce(p, [o.o_gate], take(10), 896, left=i.normed2_t, right=i.d_gate)
    up = Reduce(p, [o.o_up], [down.sent] + take(9), 896, left=i.normed2_t, right=i.d_up)
    roq = Reduce(p, [o.o_q, o.o_o], take(9), 256, src=oq)
    rkv = Reduce(p, [o.o_k, o.o_v, o.o_last], take(9), 384, src=tail, direct=True)
    firsts = [ZSum(p, i.x, total1, 128 * h, *z1[5 * h : 5 * h + 5]) for h in (0, 1)]
    x2 = total1
    second = ZSum(p, x2, total2, 0, *z2)
    wq, wk, wv, wo = [slice(c0, c0 + 256) for c0 in (0, 256, 512, 896)]
    small = i.small

    greet(
        [p.sib(), p.dy(1), p.dy(3)]
        + [p.dc(d) for d in range(1, 8)]
        + [p.dz(d) for d in (1, 2, 3)]
    )
    loads.x.wait()
    for half in firsts:
        half.start()
    for copy in loads[1:]:
        copy.wait()
    down.one()
    gate.one()
    acc[...] = jnp.zeros_like(acc)
    gt[...] = jnp.zeros_like(gt)
    hg[...] = jnp.zeros_like(hg)
    extra[...] = jnp.zeros_like(extra)
    firsts[0].middle()
    down.two()
    firsts[1].middle()
    gate.two()
    for copy in down.c1:
        copy.wait_send()
    up.one()
    for half in firsts:
        half.finish()

    @pl.loop(0, 16, unroll=4)
    def _(b):
        at = pl.ds(pl.multiple_of(b * 16, 16), 16)
        dm, dg = norm_back(
            i.middle[at, :], i.gains[2:3, :], total1[at, :].astype(F32)
        )
        acc[2] += dg
        dm = dm + i.cot[at, :].astype(F32)
        d_mid[at, :] = dm
        db, dg = norm_back(i.branch[at, :].astype(F32), i.gains[1:2, :], dm)
        acc[1] += dg
        d_branch[at, :] = db.astype(BF)

    own_pos[...] = jnp.broadcast_to(i.key_pos[p.c], (8, 256)).T[:, 0:1]
    down.three()
    d_attn[...] = plain(d_branch[...], small[:, wo]).astype(BF)
    delta[...] = jnp.sum(d_attn[...].astype(F32) * i.attn[...], axis=-1, keepdims=True)
    dq[...] = jnp.zeros_like(dq)
    up.two()

    def keys_block(kb):
        k, v = i.kv[kb, :, :HD], i.kv[kb, :, HD:]
        scores = against(i.queries[...], k) * scale
        seen = i.key_pos[kb] <= own_pos[...]
        probs = jnp.where(seen, jnp.exp(scores - i.lse[...]), 0.0)
        d_probs = against(d_attn[...], v)
        ds = (probs * (d_probs - delta[...])).astype(BF)
        dq[...] += plain(ds, k)
        dk = inner(ds, i.queries[...]) * scale
        dv = inner(probs.astype(BF), d_attn[...])
        parts[kb, :, :HD] = dk.astype(BF)
        parts[kb, :, HD:] = dv.astype(BF)

    def key_copy(kb, d, e):
        slot = 3 * (d % 8) + e - 1
        row = pl.ds(pl.multiple_of(((p.z + e) % 4) * 64, 64), 64)
        return pltpu.make_async_remote_copy(
            src_ref=parts.at[kb, row, pl.ds(0, HD)],
            dst_ref=got_k.at[e - 1, d % 8],
            send_sem=ks.at[slot],
            recv_sem=kr.at[slot],
            device_id=p.dz(e),
            device_id_type=MESH,
        )

    def value_copy(kb, d):
        return pltpu.make_async_remote_copy(
            src_ref=parts.at[kb, :, pl.ds(HD, HD)],
            dst_ref=got_v.at[d - 1],
            send_sem=vs.at[d - 1],
            recv_sem=vr.at[d - 1],
            device_id=(p.f, kb, p.z),
            device_id_type=MESH,
        )

    @pl.loop(1, 8)
    def _(d):
        kb = (p.c + d) % 8
        keys_block(kb)
        value_copy(kb, d).start()
        for e in (2, 1, 3):
            key_copy(kb, d, e).start()

    keys_block(p.c)
    for e in (2, 1, 3):
        key_copy(p.c, 0, e).start()

    down.four()
    gate.three()

    @pl.loop(0, 4)
    def _(b):
        at = pl.ds(pl.multiple_of(b * 64, 64), 64)
        dn = turn_back(dq[at, :] * scale, i.cosine[at, :], i.sine[at, :])
        dv, dg = norm_back(i.q_proj[at, :], i.heads[4:5, :], dn)
        acc[3, :, :HD] += dg.reshape(4, 16, HD).sum(axis=0)
        dq[at, :] = dv

    dq_low = dq[...].astype(BF)
    x2[...] = against(dq_low, small[:, wq]).astype(BF)
    extra[0:1, :] = jnp.sum(acc[3, :, :HD], axis=0, keepdims=True).astype(BF)
    second.start()
    more = [
        send(extra, xgot.at[d - 1], xs.at[d - 1], xr.at[d - 1], p.dz(d)) for d in (1, 2, 3)
    ]
    up.three()
    oq[:, :HD] = plain(i.normed_t[...], dq_low).astype(BF)
    oq[:, HD:] = inner(d_branch[...], i.attn_low[...]).astype(BF)
    roq.one()
    down.fourb()
    gate.four()

    for d in range(8):
        for e in (1, 2, 3):
            key_copy(p.c, d, e).wait_recv()
    own = pl.ds(pl.multiple_of(p.z * 64, 64), 64)

    @pl.loop(0, 8)
    def _(d):
        kb = (p.c + d) % 8
        total = parts[kb, own, :HD].astype(F32)
        for e in range(3):
            total = total + got_k[e, d].astype(F32)
        k_sum[d] = total.astype(BF)

    keys_far = [
        send(k_sum.at[d], far_k.at[d - 1], ks2.at[d - 1], kr2.at[d - 1], p.dc(d))
        for d in range(1, 8)
    ]
    for d in range(1, 8):
        value_copy(p.c, d).wait_recv()

    @pl.loop(0, 16, unroll=4)
    def _(b):
        at = pl.ds(pl.multiple_of(b * 16, 16), 16)
        total = parts[p.c, at, HD:].astype(F32)
        for d in range(7):
            total = total + got_v[d, at, :].astype(F32)
        v_sum[at, :] = total.astype(BF)

    values_far = [
        send(
            v_sum.at[pl.ds(pl.multiple_of(((p.z + e) % 4) * 64, 64), 64)],
            far_v.at[e - 1],
            vs2.at[e - 1],
            vr2.at[e - 1],
            p.dz(e),
        )
        for e in (2, 1, 3)
    ]
    second.middle()
    down.five()
    gate.fourb()
    roq.two()
    for copy in keys_far + values_far:
        copy.wait_recv()

    @pl.loop(0, 4)
    def _(b):
        at = pl.ds(pl.multiple_of(p.z * 64 + b * 16, 16), 16)
        to = pl.ds(pl.multiple_of(b * 16, 16), 16)
        total = k_sum[0, to, :].astype(F32)
        for d in range(7):
            total = total + far_k[d, to, :].astype(F32)
        kv_low[at, :HD] = total.astype(BF)
        total = v_sum[at, :].astype(F32)
        for e in range(3):
            total = total + far_v[e, to, :].astype(F32)
        kv_low[at, HD:] = total.astype(BF)

    kv2 = [
        send(kv_low.at[own], kv_low.at[own], os.at[d - 1], orr.at[d - 1], p.dz(d))
        for d in (2, 1, 3)
    ]
    up.four()
    down.fiveb()
    for copy in kv2:
        copy.wait_recv()
    acc[3] = jnp.zeros_like(acc[3])

    @pl.loop(0, 4)
    def _(b):
        at = pl.ds(pl.multiple_of(b * 64, 64), 64)
        dn = turn_back(kv_low[at, :HD].astype(F32), i.cosine[at, :], i.sine[at, :])
        dv, dg = norm_back(i.k_proj[at, :], i.heads[5:6, :], dn)
        acc[3, :, :HD] += dg.reshape(4, 16, HD).sum(axis=0)
        dq[at, :] = dv

    dk_low = dq[...].astype(BF)
    dn_kv[...] = against(dk_low, small[:, wk]) + against(kv_low[:, HD:], small[:, wv])
    tail[:, :HD] = plain(i.normed_t[...], dk_low).astype(BF)
    tail[:, HD : 2 * HD] = plain(i.normed_t[...], kv_low[:, HD:]).astype(BF)
    gate.five()
    up.fourb()
    roq.three()
    for copy in more:
        copy.wait()
    heads = extra[0:1, :].astype(F32)
    for d in range(3):
        heads = heads + xgot[d, 0:1, :].astype(F32)
    hg[4:5, :] = heads
    hg[5:6, :] = jnp.sum(acc[3, :, :HD], axis=0, keepdims=True)
    second.finish()

    @pl.loop(0, 16, unroll=4)
    def _(b):
        at = pl.ds(pl.multiple_of(b * 16, 16), 16)
        dn = total2[at, :].astype(F32) + dn_kv[at, :]
        dv, dg = norm_back(i.tokens[at, :].astype(F32), i.gains[0:1, :], dn)
        acc[0] += dg
        o.grad_tokens[at, :] = d_mid[at, :] + dv

    for g in range(3):
        gt[g : g + 1, :] = jnp.sum(acc[g], axis=0, keepdims=True)
    gt[3:4, :] = i.dg3[...]
    last = gt[...].T
    heads_t = hg[...].T
    tail[:, 2 * HD :] = last.astype(BF)
    for f in range(4):
        tail[288 * f : 288 * f + 64, 2 * HD :] = (
            last[288 * f : 288 * f + 64] + heads_t[64 * f : 64 * f + 64]
        ).astype(BF)
    rkv.one()
    roq.four()
    gate.fiveb()
    up.five()
    rkv.two()
    roq.fourb()
    down.six()
    rkv.three()
    up.fiveb()
    roq.five()
    rkv.four()
    rkv.fourb()
    roq.fiveb()
    gate.six()
    rkv.five()
    rkv.fiveb()
    up.six()
    roq.six()
    rkv.six()
    for d in range(8):
        for e in (1, 2, 3):
            key_copy(p.c, d, e).wait_send()
    for d in range(1, 8):
        value_copy(p.c, d).wait_send()
    for copy in kv2 + keys_far + values_far + gate.c1 + up.c1 + roq.c1 + rkv.c1:
        copy.wait_send()


def zsum_buffers(share):
    return [pltpu.VMEM((3, share, 1152), BF)] + sems(3) + sems(3)


def back_call(ins, cid):
    scratch = (
        [pltpu.VMEM(a.shape, a.dtype) for a in ins]
        + [pltpu.SemaphoreType.DMA((len(ins),))]
        + [pltpu.VMEM((256, 1152), BF), pltpu.VMEM((256, 1), F32)]
        + zsum_buffers(32) * 2
        + [pltpu.VMEM((256, 1152), BF)]
        + zsum_buffers(64)
        + [
            pltpu.VMEM((16, HD), BF),
            pltpu.VMEM((3, 16, HD), BF),
            pltpu.VMEM((256, 1152), F32),
            pltpu.VMEM((256, 1152), BF),
            pltpu.VMEM((256, HD), BF),
            pltpu.VMEM((256, 1), F32),
            pltpu.VMEM((256, HD), F32),
            pltpu.VMEM((8, 256, 2 * HD), BF),
            pltpu.VMEM((3, 8, 64, HD), BF),
            pltpu.VMEM((7, 256, HD), BF),
            pltpu.VMEM((8, 64, HD), BF),
            pltpu.VMEM((256, HD), BF),
            pltpu.VMEM((7, 64, HD), BF),
            pltpu.VMEM((3, 64, HD), BF),
            pltpu.VMEM((256, 2 * HD), BF),
            pltpu.VMEM((256, 1152), F32),
            pltpu.VMEM((4, 16, 1152), F32),
            pltpu.VMEM((128, 1152), F32),
            pltpu.VMEM((128, HD), F32),
            pltpu.VMEM((1152, 512), BF),
            pltpu.VMEM((1152, 640), BF),
        ]
        + sems(24)
        + sems(7)
        + sems(7)
        + sems(3)
        + sems(3)
        + sems(3)
        + reduce_buffers(1728, 896, True) * 2
        + reduce_buffers(1728, 896, False)
        + reduce_buffers(512, 256, False)
        + reduce_buffers(640, 384, False)
    )
    shapes = [((256, 1152), F32)] + [((288, n), BF) for n in (1728, 1728, 1728, 256, 256, 256, 256, 128)]
    return pl.pallas_call(
        back_kernel,
        out_shape=[jax.ShapeDtypeStruct(*shape) for shape in shapes],
        in_specs=[HB] * len(ins),
        out_specs=[VM] * len(shapes),
        scratch_shapes=scratch,
        compiler_params=params(cid, 62),
        name="backward",
    )(*ins)


class ForeIn(NamedTuple):
    tokens: Any
    cot: Any
    w_query: Any
    w_key: Any
    w_value: Any
    w_out: Any
    scales: Any
    head_scales: Any
    w_gate: Any
    w_up: Any
    w_down: Any
    cosine: Any
    sine: Any
    key_pos: Any

class ForeOut(NamedTuple):
    out: Any
    small: Any
    gains: Any
    heads: Any
    x: Any
    d_ffn_t: Any
    hidden: Any
    normed2_t: Any
    d_gate: Any
    d_up: Any
    middle: Any
    branch: Any
    dg3: Any
    attn: Any
    attn_low: Any
    lse: Any
    queries: Any
    kv: Any
    normed_t: Any
    q_proj: Any
    k_proj: Any

TILES = [(c0, min(c0 + 256, 1728)) for c0 in range(0, 1728, 256)]


def turn(v, cosine, sine):
    v1, v2 = v[:, :128], v[:, 128:]
    return jnp.concatenate([v1 * cosine - v2 * sine, v2 * cosine + v1 * sine], axis=1)


def transpose_into(dst, src):
    for c0 in range(0, 1152, 128):
        dst[c0 : c0 + 128, :] = src[:, c0 : c0 + 128].astype(F32).T.astype(BF)


def fore_kernel(*refs):
    n_in, n_out = len(ForeIn._fields), len(ForeOut._fields)
    i = ForeIn(*refs[:n_in])
    rest = list(refs[n_in + n_out :])

    def take(n):
        got = rest[:n]
        del rest[:n]
        return got

    o = ForeOut(*take(n_out))
    leaving = take(1)[0]
    leave = ForeOut(
        *[
            pltpu.make_async_copy(o[n], refs[n_in + n], leaving.at[n])
            for n in range(n_out)
        ]
    )
    p = Place()
    scale = HD ** (-0.5)
    w_gate, w_up, w_down, act, slope, normed, d_ffn, probs, head_cols, accg = take(10)
    local, gs, gr, ks, kr, vs, vr, fs, fr = take(9)
    total1, total2 = take(2)
    z1, z2 = take(10), take(10)
    part, pack, rows_up, own_pos = take(4)
    small = o.small
    halves = [(h, slice(128 * h, 128 * h + 128)) for h in (0, 1)]
    firsts = [ZSum(p, part, total1, 128 * h, *z1[5 * h : 5 * h + 5]) for h in (0, 1)]
    seconds = [ZSum(p, part, total2, 128 * h, *z2[5 * h : 5 * h + 5]) for h in (0, 1)]
    kv = o.kv
    gathers = [
        Gather(p, src, dst, local.at[j], gs, gr, 6 * j, 0 < j < 4)
        for j, (src, dst) in enumerate(
            [
                (pack.at[:, pl.ds(0, 896)], small.at[:, pl.ds(0, 896)]),
                (i.w_gate, w_gate),
                (i.w_up, w_up),
                (i.w_down, w_down),
                (pack.at[:, pl.ds(896, 256)], small.at[:, pl.ds(896, 256)]),
            ]
        )
    ]
    g_small, g_gate, g_up, g_down, g_out = gathers

    for ref, c0 in ((i.w_query, 0), (i.w_key, 256), (i.w_value, 512), (i.w_out, 896)):
        pack[:, c0 : c0 + 256] = ref[...]
    rows_up[...] = jnp.zeros_like(rows_up)
    rows_up[0:4, 0:288] = i.scales[...].astype(F32)
    rows_up[4:6, 0:64] = i.head_scales[...].astype(F32)
    pack[:, 768:896] = rows_up[...].T[:288, :].astype(BF)
    own_pos[...] = jnp.broadcast_to(i.key_pos[p.c], (8, 256)).T[:, 0:1]
    greet([p.sib(), p.dy(1), p.dy(3)] + [p.dc(d) for d in range(1, 8)] + [p.dz(d) for d in (1, 2, 3)])
    g_small.start()
    g_small.start_far()
    g_out.start()
    g_out.start_far()
    g_gate.start()
    g_up.start()
    g_down.start()
    accg[...] = jnp.zeros_like(accg)
    g_small.forward()
    g_gate.start_far()
    g_small.finish()

    o.gains[...] = small[:, 768:896].astype(F32).T[:8, :]
    for f in range(4):
        head_cols[64 * f : 64 * f + 64, :] = small[288 * f : 288 * f + 64, 768:896].astype(F32)
    o.heads[...] = head_cols[...].T[:8, :]
    leave.gains.start()
    leave.heads.start()

    @pl.loop(0, 16, unroll=4)
    def _(b):
        at = pl.ds(pl.multiple_of(b * 16, 16), 16)
        normed[at, :] = normalize(i.tokens[at, :].astype(F32), o.gains[0:1, :]).astype(BF)

    o.q_proj[...] = plain(normed[...], small[:, :256])
    o.k_proj[...] = plain(normed[...], small[:, 256:512])
    kv[p.c, :, HD:] = plain(normed[...], small[:, 512:768]).astype(BF)

    quarter = pl.ds(pl.multiple_of(p.z * 64, 64), 64)
    sent = [
        send(
            kv.at[p.c, quarter, pl.ds(HD, HD)],
            kv.at[p.c, quarter, pl.ds(HD, HD)],
            vs.at[d - 1],
            vr.at[d - 1],
            p.dc(d),
        )
        for d in range(1, 8)
    ]

    @pl.loop(0, 4)
    def _(b):
        at = pl.ds(pl.multiple_of(b * 64, 64), 64)
        n = normalize(o.k_proj[at, :], o.heads[5:6, :])
        kv[p.c, at, :HD] = turn(n, i.cosine[at, :], i.sine[at, :]).astype(BF)

    keys = kv.at[p.c, :, pl.ds(0, HD)]
    sent_k = [send(keys, keys, ks.at[d - 1], kr.at[d - 1], p.dc(d)) for d in range(1, 8)]

    @pl.loop(0, 4)
    def _(b):
        at = pl.ds(pl.multiple_of(b * 64, 64), 64)
        n = normalize(o.q_proj[at, :], o.heads[4:5, :])
        o.queries[at, :] = turn(n, i.cosine[at, :], i.sine[at, :]).astype(BF)

    g_out.forward()
    g_gate.across()
    g_up.start_far()
    for copy in sent:
        copy.wait_recv()
    sent_z = []
    for d in range(8):
        block = kv.at[(p.c + 8 - d) % 8, quarter, pl.ds(HD, HD)]
        if d == 0:
            continue
        sent_z += [
            send(block, block, fs.at[3 * d + e - 1], fr.at[3 * d + e - 1], p.dz(e))
            for e in (2, 1, 3)
        ]
    transpose_into(o.normed_t, normed)
    for copy in (leave.normed_t, leave.queries, leave.q_proj, leave.k_proj):
        copy.start()
    for copy in sent_k:
        copy.wait_recv()
    g_gate.forward()
    g_down.start_far()

    @pl.loop(0, 4)
    def _(b):
        at = pl.ds(pl.multiple_of(b * 64, 64), 64)
        query = o.queries[at, :]
        seen = [i.key_pos[kb] <= own_pos[at, :] for kb in range(8)]
        scores = [against(query, kv[kb, :, :HD]) * scale for kb in range(8)]
        top = jnp.max(jnp.where(seen[0], scores[0], -1e30), axis=-1, keepdims=True)
        for kb in range(1, 8):
            top = jnp.maximum(
                top, jnp.max(jnp.where(seen[kb], scores[kb], -1e30), axis=-1, keepdims=True)
            )
        scores = [jnp.where(seen[kb], jnp.exp(scores[kb] - top), 0.0) for kb in range(8)]
        total = jnp.sum(scores[0], axis=-1, keepdims=True)
        for kb in range(1, 8):
            total = total + jnp.sum(scores[kb], axis=-1, keepdims=True)
        o.lse[at, :] = top + jnp.log(total)
        share = 1.0 / total
        for kb in range(8):
            probs[kb, at, :] = (scores[kb] * share).astype(BF)

    g_up.across()
    g_out.finish()
    leave.small.start()
    for copy in sent_z:
        copy.wait_recv()
    attn = plain(probs[0], kv[0, :, HD:])
    for kb in range(1, 8):
        attn = attn + plain(probs[kb], kv[kb, :, HD:])
    o.attn[...] = attn
    attn_low = attn.astype(BF)
    o.attn_low[...] = attn_low
    for copy in (leave.kv, leave.lse, leave.attn, leave.attn_low):
        copy.start()
    for h, rows in halves:
        part[rows, :] = against(attn_low[rows], small[:, 896:]).astype(BF)
        firsts[h].start()
    g_up.forward()
    g_down.across()
    for half in firsts:
        half.middle()
    g_gate.finish()

    def middle_rows(b):
        at = pl.ds(pl.multiple_of(b * 16, 16), 16)
        branch = total1[at, :]
        o.branch[at, :] = branch
        middle = i.tokens[at, :].astype(F32) + normalize(
            branch.astype(F32), o.gains[1:2, :]
        )
        o.middle[at, :] = middle
        normed[at, :] = normalize(middle, o.gains[2:3, :]).astype(BF)

    for h, rows in halves:
        firsts[h].finish()
        pl.loop(8 * h, 8 * h + 8, unroll=4)(middle_rows)
    g_up.finish()
    leave.branch.start()
    leave.middle.start()
    for c0, c1 in TILES:
        gate = plain(normed[...], w_gate[:, c0:c1])
        up = plain(normed[...], w_up[:, c0:c1])
        bend = jnp.tanh(0.7978845608028654 * (gate + 0.044715 * gate * gate * gate))
        gelu = 0.5 * gate * (1.0 + bend)
        o.hidden[:, c0:c1] = (gelu * up).astype(BF)
        act[:, c0:c1] = gelu
        rise = 0.7978845608028654 * (1.0 + 0.134145 * gate * gate)
        slope[:, c0:c1] = up * (0.5 * (1.0 + bend) + 0.5 * gate * (1.0 - bend * bend) * rise)
    leave.hidden.start()
    g_down.forward()
    g_down.finish()
    for h, rows in halves:
        for c0 in range(0, 1152, 384):
            part[rows, c0 : c0 + 384] = against(
                o.hidden[rows, :], w_down[c0 : c0 + 384, :]
            ).astype(BF)
        seconds[h].start()
    transpose_into(o.normed2_t, normed)
    leave.normed2_t.start()
    for half in seconds:
        half.middle()

    def last_rows(b):
        at = pl.ds(pl.multiple_of(b * 16, 16), 16)
        ffn = total2[at, :].astype(F32)
        o.out[at, :] = (o.middle[at, :] + normalize(ffn, o.gains[3:4, :])).astype(BF)
        dv, dg = norm_back(ffn, o.gains[3:4, :], i.cot[at, :].astype(F32))
        accg[...] += dg
        d_ffn[at, :] = dv.astype(BF)

    for h, rows in halves:
        seconds[h].finish()
        pl.loop(8 * h, 8 * h + 8, unroll=4)(last_rows)
    o.dg3[...] = jnp.sum(accg[...], axis=0, keepdims=True)
    transpose_into(o.d_ffn_t, d_ffn)
    for copy in (leave.out, leave.dg3, leave.d_ffn_t):
        copy.start()
    for c0, c1 in TILES:
        d_hidden = plain(d_ffn[...], w_down[:, c0:c1])
        o.d_up[:, c0:c1] = (d_hidden * act[:, c0:c1]).astype(BF)
        o.d_gate[:, c0:c1] = (d_hidden * slope[:, c0:c1]).astype(BF)
    leave.d_up.start()
    leave.d_gate.start()
    for c0 in range(0, 1152, 384):
        o.x[:, c0 : c0 + 384] = (
            against(o.d_gate[...], w_gate[c0 : c0 + 384, :])
            + against(o.d_up[...], w_up[c0 : c0 + 384, :])
        ).astype(BF)
    leave.x.start()
    for copy in leave:
        copy.wait()
    for copy in sent + sent_k + sent_z:
        copy.wait_send()


def fore_call(ins, cid):
    shapes = ForeOut(
        out=((256, 1152), BF),
        small=((1152, 1152), BF),
        gains=((8, 1152), F32),
        heads=((8, 256), F32),
        x=((256, 1152), BF),
        d_ffn_t=((1152, 256), BF),
        hidden=((256, 1728), BF),
        normed2_t=((1152, 256), BF),
        d_gate=((256, 1728), BF),
        d_up=((256, 1728), BF),
        middle=((256, 1152), F32),
        branch=((256, 1152), BF),
        dg3=((1, 1152), F32),
        attn=((256, 256), F32),
        attn_low=((256, 256), BF),
        lse=((256, 1), F32),
        queries=((256, 256), BF),
        kv=((8, 256, 512), BF),
        normed_t=((1152, 256), BF),
        q_proj=((256, 256), F32),
        k_proj=((256, 256), F32),
    )
    scratch = (
        [pltpu.VMEM(*shape) for shape in shapes]
        + [pltpu.SemaphoreType.DMA((len(shapes),))]
        + [pltpu.VMEM((1152, 1728), BF)] * 3
        + [
            pltpu.VMEM((256, 1728), F32),
            pltpu.VMEM((256, 1728), F32),
            pltpu.VMEM((256, 1152), BF),
            pltpu.VMEM((256, 1152), BF),
            pltpu.VMEM((8, 256, 256), BF),
            pltpu.VMEM((256, 128), F32),
            pltpu.VMEM((16, 1152), F32),
            pltpu.SemaphoreType.DMA((5,)),
        ]
        + sems(30)
        + sems(7)
        + sems(7)
        + sems(24)
        + [pltpu.VMEM((256, 1152), BF)] * 2
        + zsum_buffers(32) * 4
        + [pltpu.VMEM((256, 1152), BF), pltpu.VMEM((288, 1152), BF)]
        + [pltpu.VMEM((128, 384), F32), pltpu.VMEM((256, 1), F32)]
    )
    done = pl.pallas_call(
        fore_kernel,
        out_shape=[jax.ShapeDtypeStruct(*shape) for shape in shapes],
        in_specs=[HB if a.shape == (288, 1728) else VM for a in ins],
        out_specs=[HB] * len(shapes),
        scratch_shapes=scratch,
        compiler_params=params(cid, 62),
        name="forward",
    )(*ins)
    return ForeOut(*done)


def final_kernel(*refs):
    ins, outs = refs[:10], refs[10:21]
    held, wide, (rows_ref, heads_ref, s_in, s_out) = refs[21:31], refs[31:38], refs[38:]
    loads = [pltpu.make_async_copy(ins[n], held[n], s_in.at[n]) for n in range(10)]
    for copy in loads:
        copy.start()
    stores = []
    for n in range(9):
        loads[n].wait()
        if n > 1:
            wide[n - 2][...] = held[n][...].astype(F32)
        copy = pltpu.make_async_copy(held[n] if n < 2 else wide[n - 2], outs[n], s_out.at[n])
        copy.start()
        stores.append(copy)
    loads[9].wait()
    columns = held[9][...].astype(F32).T
    rows_ref[...] = columns[:4, :]
    heads_ref[...] = columns[4:6, :64]
    for n, ref in ((9, rows_ref), (10, heads_ref)):
        copy = pltpu.make_async_copy(ref, outs[n], s_out.at[n])
        copy.start()
        stores.append(copy)
    for copy in stores:
        copy.wait()


def final_call(*ins):
    grads = [a.shape for a in ins[2:9]]
    shapes = [ins[0].shape, ins[1].shape] + grads + [(4, 288), (2, 64)]
    any_space = pl.BlockSpec(memory_space=pl.ANY)
    return pl.pallas_call(
        final_kernel,
        out_shape=[
            jax.ShapeDtypeStruct(shape, BF if n == 0 else F32) for n, shape in enumerate(shapes)
        ],
        in_specs=[any_space] * 10,
        out_specs=[any_space] * 11,
        scratch_shapes=[pltpu.VMEM(a.shape, a.dtype) for a in ins]
        + [pltpu.VMEM(shape, F32) for shape in grads]
        + [
            pltpu.VMEM((4, 288), F32),
            pltpu.VMEM((2, 64), F32),
            pltpu.SemaphoreType.DMA((10,)),
            pltpu.SemaphoreType.DMA((11,)),
        ],
        compiler_params=pltpu.CompilerParams(vmem_limit_bytes=62 * 2**20),
        name="final",
    )(*ins)


def per_device(
    tokens,
    block_order,
    cotangent,
    w_query,
    w_key,
    w_value,
    w_out,
    w_gate,
    w_up,
    w_down,
    gains,
    head_gains,
):
    _, rows, width = tokens.shape
    cycle_index = lax.axis_index("context")
    span = rows // 2
    seq_len = rows * 8

    offsets = jnp.arange(seq_len, dtype=jnp.int32)
    key_pos = (jnp.repeat(block_order, span, axis=1) * span + (offsets % span)[None, :])[0]
    query_pos = lax.dynamic_slice_in_dim(key_pos, cycle_index * rows, rows, 0)
    cosine, sine = tables(query_pos)
    ins = ForeIn(
        tokens=tokens[0],
        cot=cotangent[0],
        w_query=w_query,
        w_key=w_key,
        w_value=w_value,
        w_out=w_out.T,
        scales=gains,
        head_scales=head_gains,
        w_gate=w_gate,
        w_up=w_up,
        w_down=w_down.T,
        cosine=cosine,
        sine=sine,
        key_pos=key_pos.astype(F32).reshape(8, 1, rows),
    )
    held = fore_call(ins, 1)
    grad_tokens, sum_down, sum_gate, sum_up, sum_q, sum_o, sum_k, sum_v, last = back_call(
        BackIn(
            x=held.x,
            d_ffn_t=held.d_ffn_t,
            hidden=held.hidden,
            normed2_t=held.normed2_t,
            d_gate=held.d_gate,
            d_up=held.d_up,
            middle=held.middle,
            branch=held.branch,
            cot=ins.cot,
            tokens=ins.tokens,
            gains=held.gains,
            dg3=held.dg3,
            attn=held.attn,
            attn_low=held.attn_low,
            lse=held.lse,
            queries=held.queries,
            kv=held.kv,
            key_pos=ins.key_pos,
            small=held.small,
            normed_t=held.normed_t,
            q_proj=held.q_proj,
            k_proj=held.k_proj,
            heads=held.heads,
            cosine=ins.cosine,
            sine=ins.sine,
        ),
        2,
    )
    done = final_call(
        held.out, grad_tokens, sum_gate, sum_up, sum_down, sum_q, sum_k, sum_v, sum_o, last
    )
    result, d_tokens, d_gate, d_up, d_down, d_q, d_k, d_v, d_o, d_gains, d_heads = done
    return (
        result[None],
        d_tokens[None],
        d_q,
        d_k,
        d_v,
        d_o.T,
        d_gate,
        d_up,
        d_down.T,
        d_gains,
        d_heads,
    )


def solution(mesh):
    in_specs = (
        P("fsdp", "context", None),
        P("fsdp", None),
        P("fsdp", "context", None),
        P("fsdp", "tensor"),
        P("fsdp", None),
        P("fsdp", None),
        P("tensor", "fsdp"),
        P("fsdp", "tensor"),
        P("fsdp", "tensor"),
        P("tensor", "fsdp"),
        P(None, "fsdp"),
        P(None, "fsdp"),
    )
    out_specs = (
        P("fsdp", "context", None),
        P("fsdp", "context", None),
        P("fsdp", "tensor"),
        P("fsdp", None),
        P("fsdp", None),
        P("tensor", "fsdp"),
        P("fsdp", "tensor"),
        P("fsdp", "tensor"),
        P("tensor", "fsdp"),
        P(None, "fsdp"),
        P(None, "fsdp"),
    )
    return jax.shard_map(
        per_device, mesh=mesh, in_specs=in_specs, out_specs=out_specs, check_vma=False
    )
```

```python
import functools
import math
from typing import Any, NamedTuple

import jax
import jax.numpy as jnp
from jax import lax
from jax.experimental import pallas as pl
from jax.experimental.pallas import tpu as pltpu
from jax.sharding import PartitionSpec as P

HD = 256
ROPE_BASE = 1000000.0
EPS = 1e-06
MESH = pl.DeviceIdType.MESH
BF = jnp.bfloat16
F32 = jnp.float32


def normalize(values, gain):
    return values * lax.rsqrt(jnp.mean(values * values, axis=-1, keepdims=True) + EPS) * gain


def rotate(values, cosine, sine):
    middle = values.shape[-1] // 2
    first = values[..., :middle]
    second = values[..., middle:]
    return jnp.concatenate(
        [first * cosine - second * sine, second * cosine + first * sine], axis=-1
    )


def tables(positions):
    steps = jnp.arange(HD // 2, dtype=jnp.float32) * (2.0 / HD)
    inverse = jnp.exp(-math.log(ROPE_BASE) * steps)
    angle = positions.astype(jnp.float32)[:, None] * inverse[None, :]
    return (jnp.cos(angle), jnp.sin(angle))


def plain(left, right):
    return jnp.dot(left, right, preferred_element_type=jnp.float32)


def inner(left, right):
    return lax.dot_general(
        left, right, (((0,), (0,)), ((), ())), preferred_element_type=jnp.float32
    )


def against(left, right):
    return lax.dot_general(
        left, right, (((1,), (1,)), ((), ())), preferred_element_type=jnp.float32
    )


class Place:
    def __init__(self):
        f = lax.axis_index("fsdp")
        c = lax.axis_index("context")
        self.f, self.c, self.z = f, c, lax.axis_index("tensor")
        self.ylo, self.core = f // 2, f % 2
        self.x, self.yhi = c // 2, c % 2
        self.y = self.yhi * 2 + self.ylo

    def at(self, x=None, y=None, z=None, core=None):
        x = self.x if x is None else x
        y = self.y if y is None else y
        z = self.z if z is None else z
        core = self.core if core is None else core
        return ((y % 2) * 2 + core, x * 2 + y // 2, z)

    def sib(self):
        return self.at(core=1 - self.core)

    def dy(self, d):
        return self.at(y=(self.y + d) % 4)

    def dx(self, d):
        return self.at(x=(self.x + d) % 4)

    def dz(self, d):
        return self.at(z=(self.z + d) % 4)

    def dc(self, d):
        return (self.f, (self.c + d) % 8, self.z)


def greet(devices):
    barrier = pltpu.get_barrier_semaphore()
    for device in devices:
        pl.semaphore_signal(barrier, inc=1, device_id=device, device_id_type=MESH)
    pl.semaphore_wait(barrier, len(devices))


def send(src, dst, ssem, rsem, device):
    copy = pltpu.make_async_remote_copy(
        src_ref=src, dst_ref=dst, send_sem=ssem, recv_sem=rsem, device_id=device, device_id_type=MESH
    )
    copy.start()
    return copy


def sems(n):
    return [pltpu.SemaphoreType.DMA((n,)), pltpu.SemaphoreType.DMA((n,))]


VM = pl.BlockSpec(memory_space=pltpu.VMEM)
HB = pl.BlockSpec(memory_space=pl.ANY)


def params(cid, limit=48):
    return pltpu.CompilerParams(
        collective_id=cid, has_side_effects=True, vmem_limit_bytes=limit * 2**20
    )


class Gather:
    def __init__(self, place, src, out, local, ssem, rsem, base, relay=False):
        self.p, self.src, self.out = place, src, out
        self.local, self.ssem, self.rsem, self.base = local, ssem, rsem, base
        self.rows, self.relay = src.shape[0], relay

    def go(self, n, src, dst, device):
        return send(src, dst, self.ssem.at[self.base + n], self.rsem.at[self.base + n], device)

    def at(self, row, n):
        return self.out.at[pl.ds(pl.multiple_of(row, 16), n)]

    def start(self):
        p, rows = self.p, self.rows
        own = self.at(p.f * rows, rows)
        self.s = self.go(2, self.src, own, p.sib())
        self.l = pltpu.make_async_copy(self.src, own, self.local)
        self.l.start()

    def start_far(self):
        p, rows, half = self.p, self.rows, self.rows // 2
        first, n = (64 * (p.x % 2), 80) if self.relay else (0, half)
        self.y = []
        for h, d in ((0, 1), (1, 3)):
            row = first + half * h
            src = self.src.at[pl.ds(pl.multiple_of(row, 16), n)]
            self.y.append(self.go(h, src, self.at(p.f * rows + row, n), p.dy(d)))

    def across(self):
        p, half = self.p, self.rows // 2
        for copy in self.y:
            copy.wait_recv()
        row = (2 * (1 - p.ylo) + p.core) * self.rows
        flip, back = p.x + 1 - 2 * (p.x % 2), 3 - p.x
        self.w = []
        for h, x in ((0, flip), (1, back)):
            part = self.at(row + half * h + 80 * (p.x % 2), 64)
            self.w.append(self.go(4 + h, part, part, p.at(x=x)))

    def forward(self):
        p, rows = self.p, self.rows
        for copy in self.w if self.relay else self.y:
            copy.wait_recv()
        block = self.at((2 * (1 - p.ylo) + p.core) * rows, rows)
        self.t = self.go(3, block, block, p.sib())

    def finish(self):
        self.l.wait()
        for copy in self.y:
            copy.wait_send()
        if self.relay:
            for copy in self.w:
                copy.wait_send()
        self.s.wait()
        self.t.wait()


class ZSum:
    def __init__(self, place, x, out, base, got, s1, r1, s2, r2):
        self.p, self.x, self.got, self.out = place, x, got, out
        self.base, self.share = base, got.shape[1]
        self.s1, self.r1, self.s2, self.r2 = s1, r1, s2, r2

    def rows(self, block):
        return pl.ds(pl.multiple_of(self.base + block * self.share, 32), self.share)

    def start(self):
        p = self.p
        self.c1 = [
            send(
                self.x.at[self.rows((p.z + d) % 4)],
                self.got.at[d - 1],
                self.s1.at[d - 1],
                self.r1.at[d - 1],
                p.dz(d),
            )
            for d in (2, 1, 3)
        ]

    def middle(self):
        p = self.p
        for copy in self.c1:
            copy.wait_recv()
        own = self.rows(p.z)

        @pl.loop(0, self.share // 16, unroll=2)
        def _(i):
            at = pl.ds(pl.multiple_of(self.base + p.z * self.share + i * 16, 16), 16)
            to = pl.ds(pl.multiple_of(i * 16, 16), 16)
            total = self.x[at, :].astype(F32)
            for d in range(3):
                total = total + self.got[d, to, :].astype(F32)
            self.out[at, :] = total.astype(BF)

        self.c2 = [
            send(self.out.at[own], self.out.at[own], self.s2.at[d - 1], self.r2.at[d - 1], p.dz(d))
            for d in (2, 1, 3)
        ]

    def finish(self):
        for copy in self.c1:
            copy.wait_send()
        for copy in self.c2:
            copy.wait()


class Reduce:
    def __init__(self, place, out, bufs, cut, src=None, left=None, right=None, direct=False):
        self.p, self.src, self.left, self.right = place, src, left, right
        self.outs, self.cut = out, cut
        if src is None:
            self.sent, bufs = bufs[0], bufs[1:]
        self.r1, self.r2, self.q, self.r3, self.r4, self.r5, self.r6, self.s, self.r = bufs
        self.n = sum(ref.shape[1] for ref in out)
        self.ns, self.direct = 0, direct
        x, side = place.x, (cut // 128 + 1) // 2 * 128
        flip, back = x + 1 - 2 * (x % 2), 3 - x
        self.ways = [
            (flip, back, 3 - flip, pl.ds(0, side)),
            (back, flip, back + 1 - 2 * (back % 2), pl.ds(side, cut - side)),
        ]

    def go(self, src, dst, device):
        i = self.ns
        self.ns += 1
        return send(src, dst, self.s.at[i], self.r.at[i], device)

    def rows(self, block):
        return pl.ds(pl.multiple_of(block * 288, 16), 288)

    def product(self, block, c0, c1):
        return plain(self.left[self.rows(block), :], self.right[:, c0:c1])

    def tiles(self):
        return [(c0, min(c0 + 256, self.n)) for c0 in range(0, self.n, 256)]

    def one(self):
        p = self.p
        if self.src is None:

            @pl.loop(0, 2)
            def _(j):
                for c0, c1 in self.tiles():
                    self.sent[j, :, c0:c1] = self.product(2 * j + 1 - p.core, c0, c1).astype(BF)

            blocks = [self.sent.at[j] for j in (0, 1)]
        else:
            blocks = [self.src.at[self.rows(2 * j + 1 - p.core)] for j in (0, 1)]
        self.c1 = [self.go(blocks[j], self.r1.at[j], p.sib()) for j in (0, 1)]

    def two(self):
        p = self.p
        for copy in self.c1:
            copy.wait_recv()
        if self.src is None:

            @pl.loop(0, 2)
            def _(j):
                for c0, c1 in self.tiles():
                    self.r1[j, :, c0:c1] = (
                        self.product(2 * j + p.core, c0, c1) + self.r1[j, :, c0:c1].astype(F32)
                    ).astype(BF)

        else:

            @pl.loop(0, 18, unroll=3)
            def _(i):
                at = pl.ds(pl.multiple_of(i * 16, 16), 16)
                for j in (0, 1):
                    row = pl.multiple_of((2 * j + p.core) * 288 + i * 16, 16)
                    own = self.src[pl.ds(row, 16), :]
                    self.r1[j, at, :] = (own.astype(F32) + self.r1[j, at, :].astype(F32)).astype(BF)

        far = 1 - p.ylo
        self.c2 = [
            self.go(self.r1.at[far, pl.ds(0, 144)], self.r2.at[pl.ds(0, 144)], p.dy(1)),
            self.go(self.r1.at[far, pl.ds(144, 144)], self.r2.at[pl.ds(144, 144)], p.dy(3)),
        ]

    def three(self):
        p, cut = self.p, self.cut
        for copy in self.c2:
            copy.wait_recv()
        rest = self.n - cut

        @pl.loop(0, 9, unroll=3)
        def _(i):
            for h in (0, 1):
                at = pl.ds(pl.multiple_of(h * 144 + i * 16, 16), 16)
                to = pl.ds(pl.multiple_of(i * 16, 16), 16)
                total = (self.r1[p.ylo, at, :].astype(F32) + self.r2[at, :].astype(F32)).astype(BF)
                self.q[2 * h, to, :] = total[:, :cut]
                if rest == cut:
                    self.q[2 * h + 1, to, :] = total[:, cut:]
                else:
                    self.q[2 * h + 1, to, :] = jnp.concatenate(
                        [total[:, cut:], jnp.zeros((16, cut - rest), BF)], axis=1
                    )

        if self.direct:
            self.c3 = [
                self.go(self.q.at[(p.x + d) % 4], self.r3.at[d - 1], p.dx(d)) for d in (2, 1, 3)
            ]
            return
        self.c3 = []
        for one, two, theirs, cols in self.ways:
            for k, quarter in enumerate((one, theirs)):
                self.c3.append(
                    self.go(self.q.at[quarter, :, cols], self.r3.at[k, :, cols], p.at(x=one))
                )

    def sum_rows(self, dst, first, *more):
        @pl.loop(0, 9, unroll=3)
        def _(i):
            at = pl.ds(pl.multiple_of(i * 16, 16), 16)
            total = first[at, :].astype(F32)
            for ref in more:
                total = total + ref[at, :].astype(F32)
            dst[at, :] = total.astype(BF)

    def four(self):
        p = self.p
        for copy in self.c3:
            copy.wait_recv()
        if self.direct:
            return
        mine = self.q.at[p.x]
        self.sum_rows(mine, mine, self.r3.at[0])
        self.c3b = []
        for one, two, _, cols in self.ways:
            held = self.q.at[two, :, cols]
            self.sum_rows(held, held, self.r3.at[1, :, cols])
            self.c3b.append(self.go(held, self.r3.at[2, :, cols], p.at(x=two)))

    def fourb(self):
        p = self.p
        if self.direct:
            self.sum_rows(self.r6, self.q.at[p.x], *[self.r3.at[d] for d in range(3)])
        else:
            for copy in self.c3b:
                copy.wait_recv()
            self.sum_rows(self.r6, self.q.at[p.x], self.r3.at[2])
        self.c4 = self.go(self.r6, self.r4, p.dy(2))

    def five(self):
        p = self.p
        self.c4.wait()
        mine = self.r5.at[p.x]
        self.sum_rows(mine, self.r6, self.r4)
        if self.direct:
            self.c5 = [self.go(mine, mine, p.dx(d)) for d in (2, 1, 3)]
            return
        self.c5 = []
        for one, two, _, cols in self.ways:
            part = self.r5.at[p.x, :, cols]
            self.c5.append(self.go(part, part, p.at(x=two)))
            self.c5.append(self.go(part, part, p.at(x=one)))

    def fiveb(self):
        p = self.p
        self.c5b = []
        if self.direct:
            return
        for k, (one, two, _, cols) in enumerate(self.ways):
            self.c5[2 * k].wait_recv()
            part = self.r5.at[two, :, cols]
            self.c5b.append(self.go(part, part, p.at(x=one)))

    def put(self, rows, c0, value):
        start = 0
        for ref in self.outs:
            end = start + ref.shape[1]
            lo, hi = max(c0, start), min(c0 + value.shape[1], end)
            if lo < hi:
                ref[rows, lo - start : hi - start] = value[:, lo - c0 : hi - c0]
            start = end

    def six(self):
        rest = self.n - self.cut
        for copy in self.c5b + (self.c5 if self.direct else self.c5[1::2]):
            copy.wait_recv()

        @pl.loop(0, 9, unroll=3)
        def _(i):
            at = pl.ds(pl.multiple_of(i * 16, 16), 16)
            for h in (0, 1):
                to = pl.ds(pl.multiple_of(h * 144 + i * 16, 16), 16)
                self.put(to, 0, self.r5[2 * h, at, :])
                self.put(to, self.cut, self.r5[2 * h + 1, at, :rest])

        for copy in self.c2 + self.c3 + self.c5 + self.c5b:
            copy.wait_send()
        if not self.direct:
            for copy in self.c3b:
                copy.wait_send()


def reduce_buffers(n, cut, computed):
    bufs = [
        pltpu.VMEM((2, 288, n), BF),
        pltpu.VMEM((288, n), BF),
        pltpu.VMEM((4, 144, cut), BF),
        pltpu.VMEM((3, 144, cut), BF),
        pltpu.VMEM((144, cut), BF),
        pltpu.VMEM((4, 144, cut), BF),
        pltpu.VMEM((144, cut), BF),
    ] + sems(20)
    return [pltpu.VMEM((2, 288, n), BF)] + bufs if computed else bufs


def norm_back(v, gain, dy):
    r = lax.rsqrt(jnp.mean(v * v, axis=-1, keepdims=True) + EPS)
    gdy = gain * dy
    dv = r * gdy - v * (r * r * r * jnp.mean(gdy * v, axis=-1, keepdims=True))
    return dv, r * v * dy


def turn_back(d, cosine, sine):
    d1, d2 = d[:, :128], d[:, 128:]
    return jnp.concatenate([d1 * cosine + d2 * sine, d2 * cosine - d1 * sine], axis=1)


class BackIn(NamedTuple):
    x: Any
    d_ffn_t: Any
    hidden: Any
    normed2_t: Any
    d_gate: Any
    d_up: Any
    middle: Any
    branch: Any
    cot: Any
    tokens: Any
    gains: Any
    dg3: Any
    attn: Any
    attn_low: Any
    lse: Any
    queries: Any
    kv: Any
    key_pos: Any
    small: Any
    normed_t: Any
    q_proj: Any
    k_proj: Any
    heads: Any
    cosine: Any
    sine: Any

class BackOut(NamedTuple):
    grad_tokens: Any
    o_down: Any
    o_gate: Any
    o_up: Any
    o_q: Any
    o_o: Any
    o_k: Any
    o_v: Any
    o_last: Any


def back_kernel(*refs):
    n_in, n_out = len(BackIn._fields), len(BackOut._fields)
    o = BackOut(*refs[n_in : n_in + n_out])
    rest = list(refs[n_in + n_out :])

    def take(n):
        got = rest[:n]
        del rest[:n]
        return got

    i = BackIn(*take(n_in))
    loading = take(1)[0]
    loads = BackIn(
        *[pltpu.make_async_copy(refs[n], i[n], loading.at[n]) for n in range(n_in)]
    )
    for copy in loads:
        copy.start()
    p = Place()
    scale = HD ** (-0.5)
    total1 = take(1)[0]
    own_pos = take(1)[0]
    z1 = take(10)
    total2 = take(1)[0]
    z2 = take(5)
    (extra, xgot, d_mid, d_branch, d_attn, delta, dq, parts) = take(8)
    got_k, got_v, k_sum, v_sum, far_k, far_v = take(6)
    (kv_low, dn_kv, acc, gt, hg, oq, tail) = take(7)
    ks, kr, vs, vr, ks2, kr2, vs2, vr2, os, orr, xs, xr = take(12)
    down = Reduce(p, [o.o_down], take(10), 896, left=i.d_ffn_t, right=i.hidden)
    gate = Reduce(p, [o.o_gate], take(10), 896, left=i.normed2_t, right=i.d_gate)
    up = Reduce(p, [o.o_up], [down.sent] + take(9), 896, left=i.normed2_t, right=i.d_up)
    roq = Reduce(p, [o.o_q, o.o_o], take(9), 256, src=oq)
    rkv = Reduce(p, [o.o_k, o.o_v, o.o_last], take(9), 384, src=tail, direct=True)
    firsts = [ZSum(p, i.x, total1, 128 * h, *z1[5 * h : 5 * h + 5]) for h in (0, 1)]
    x2 = total1
    second = ZSum(p, x2, total2, 0, *z2)
    wq, wk, wv, wo = [slice(c0, c0 + 256) for c0 in (0, 256, 512, 896)]
    small = i.small

    greet(
        [p.sib(), p.dy(1), p.dy(3)]
        + [p.dc(d) for d in range(1, 8)]
        + [p.dz(d) for d in (1, 2, 3)]
    )
    loads.x.wait()
    for half in firsts:
        half.start()
    for copy in loads[1:]:
        copy.wait()
    down.one()
    gate.one()
    acc[...] = jnp.zeros_like(acc)
    gt[...] = jnp.zeros_like(gt)
    hg[...] = jnp.zeros_like(hg)
    extra[...] = jnp.zeros_like(extra)
    firsts[0].middle()
    down.two()
    firsts[1].middle()
    gate.two()
    for copy in down.c1:
        copy.wait_send()
    up.one()
    for half in firsts:
        half.finish()

    @pl.loop(0, 16, unroll=4)
    def _(b):
        at = pl.ds(pl.multiple_of(b * 16, 16), 16)
        dm, dg = norm_back(
            i.middle[at, :], i.gains[2:3, :], total1[at, :].astype(F32)
        )
        acc[2] += dg
        dm = dm + i.cot[at, :].astype(F32)
        d_mid[at, :] = dm
        db, dg = norm_back(i.branch[at, :].astype(F32), i.gains[1:2, :], dm)
        acc[1] += dg
        d_branch[at, :] = db.astype(BF)

    own_pos[...] = jnp.broadcast_to(i.key_pos[p.c], (8, 256)).T[:, 0:1]
    down.three()
    d_attn[...] = plain(d_branch[...], small[:, wo]).astype(BF)
    delta[...] = jnp.sum(d_attn[...].astype(F32) * i.attn[...], axis=-1, keepdims=True)
    dq[...] = jnp.zeros_like(dq)
    up.two()

    def keys_block(kb):
        k, v = i.kv[kb, :, :HD], i.kv[kb, :, HD:]
        scores = against(i.queries[...], k) * scale
        seen = i.key_pos[kb] <= own_pos[...]
        probs = jnp.where(seen, jnp.exp(scores - i.lse[...]), 0.0)
        d_probs = against(d_attn[...], v)
        ds = (probs * (d_probs - delta[...])).astype(BF)
        dq[...] += plain(ds, k)
        dk = inner(ds, i.queries[...]) * scale
        dv = inner(probs.astype(BF), d_attn[...])
        parts[kb, :, :HD] = dk.astype(BF)
        parts[kb, :, HD:] = dv.astype(BF)

    def key_copy(kb, d, e):
        slot = 3 * (d % 8) + e - 1
        row = pl.ds(pl.multiple_of(((p.z + e) % 4) * 64, 64), 64)
        return pltpu.make_async_remote_copy(
            src_ref=parts.at[kb, row, pl.ds(0, HD)],
            dst_ref=got_k.at[e - 1, d % 8],
            send_sem=ks.at[slot],
            recv_sem=kr.at[slot],
            device_id=p.dz(e),
            device_id_type=MESH,
        )

    def value_copy(kb, d):
        return pltpu.make_async_remote_copy(
            src_ref=parts.at[kb, :, pl.ds(HD, HD)],
            dst_ref=got_v.at[d - 1],
            send_sem=vs.at[d - 1],
            recv_sem=vr.at[d - 1],
            device_id=(p.f, kb, p.z),
            device_id_type=MESH,
        )

    @pl.loop(1, 8)
    def _(d):
        kb = (p.c + d) % 8
        keys_block(kb)
        value_copy(kb, d).start()
        for e in (2, 1, 3):
            key_copy(kb, d, e).start()

    keys_block(p.c)
    for e in (2, 1, 3):
        key_copy(p.c, 0, e).start()

    down.four()
    gate.three()

    @pl.loop(0, 4)
    def _(b):
        at = pl.ds(pl.multiple_of(b * 64, 64), 64)
        dn = turn_back(dq[at, :] * scale, i.cosine[at, :], i.sine[at, :])
        dv, dg = norm_back(i.q_proj[at, :], i.heads[4:5, :], dn)
        acc[3, :, :HD] += dg.reshape(4, 16, HD).sum(axis=0)
        dq[at, :] = dv

    dq_low = dq[...].astype(BF)
    x2[...] = against(dq_low, small[:, wq]).astype(BF)
    extra[0:1, :] = jnp.sum(acc[3, :, :HD], axis=0, keepdims=True).astype(BF)
    second.start()
    more = [
        send(extra, xgot.at[d - 1], xs.at[d - 1], xr.at[d - 1], p.dz(d)) for d in (1, 2, 3)
    ]
    up.three()
    oq[:, :HD] = plain(i.normed_t[...], dq_low).astype(BF)
    oq[:, HD:] = inner(d_branch[...], i.attn_low[...]).astype(BF)
    roq.one()
    down.fourb()
    gate.four()

    for d in range(8):
        for e in (1, 2, 3):
            key_copy(p.c, d, e).wait_recv()
    own = pl.ds(pl.multiple_of(p.z * 64, 64), 64)

    @pl.loop(0, 8)
    def _(d):
        kb = (p.c + d) % 8
        total = parts[kb, own, :HD].astype(F32)
        for e in range(3):
            total = total + got_k[e, d].astype(F32)
        k_sum[d] = total.astype(BF)

    keys_far = [
        send(k_sum.at[d], far_k.at[d - 1], ks2.at[d - 1], kr2.at[d - 1], p.dc(d))
        for d in range(1, 8)
    ]
    for d in range(1, 8):
        value_copy(p.c, d).wait_recv()

    @pl.loop(0, 16, unroll=4)
    def _(b):
        at = pl.ds(pl.multiple_of(b * 16, 16), 16)
        total = parts[p.c, at, HD:].astype(F32)
        for d in range(7):
            total = total + got_v[d, at, :].astype(F32)
        v_sum[at, :] = total.astype(BF)

    values_far = [
        send(
            v_sum.at[pl.ds(pl.multiple_of(((p.z + e) % 4) * 64, 64), 64)],
            far_v.at[e - 1],
            vs2.at[e - 1],
            vr2.at[e - 1],
            p.dz(e),
        )
        for e in (2, 1, 3)
    ]
    second.middle()
    down.five()
    gate.fourb()
    roq.two()
    for copy in keys_far + values_far:
        copy.wait_recv()

    @pl.loop(0, 4)
    def _(b):
        at = pl.ds(pl.multiple_of(p.z * 64 + b * 16, 16), 16)
        to = pl.ds(pl.multiple_of(b * 16, 16), 16)
        total = k_sum[0, to, :].astype(F32)
        for d in range(7):
            total = total + far_k[d, to, :].astype(F32)
        kv_low[at, :HD] = total.astype(BF)
        total = v_sum[at, :].astype(F32)
        for e in range(3):
            total = total + far_v[e, to, :].astype(F32)
        kv_low[at, HD:] = total.astype(BF)

    kv2 = [
        send(kv_low.at[own], kv_low.at[own], os.at[d - 1], orr.at[d - 1], p.dz(d))
        for d in (2, 1, 3)
    ]
    up.four()
    down.fiveb()
    for copy in kv2:
        copy.wait_recv()
    acc[3] = jnp.zeros_like(acc[3])

    @pl.loop(0, 4)
    def _(b):
        at = pl.ds(pl.multiple_of(b * 64, 64), 64)
        dn = turn_back(kv_low[at, :HD].astype(F32), i.cosine[at, :], i.sine[at, :])
        dv, dg = norm_back(i.k_proj[at, :], i.heads[5:6, :], dn)
        acc[3, :, :HD] += dg.reshape(4, 16, HD).sum(axis=0)
        dq[at, :] = dv

    dk_low = dq[...].astype(BF)
    dn_kv[...] = against(dk_low, small[:, wk]) + against(kv_low[:, HD:], small[:, wv])
    tail[:, :HD] = plain(i.normed_t[...], dk_low).astype(BF)
    tail[:, HD : 2 * HD] = plain(i.normed_t[...], kv_low[:, HD:]).astype(BF)
    gate.five()
    up.fourb()
    roq.three()
    for copy in more:
        copy.wait()
    heads = extra[0:1, :].astype(F32)
    for d in range(3):
        heads = heads + xgot[d, 0:1, :].astype(F32)
    hg[4:5, :] = heads
    hg[5:6, :] = jnp.sum(acc[3, :, :HD], axis=0, keepdims=True)
    second.finish()

    @pl.loop(0, 16, unroll=4)
    def _(b):
        at = pl.ds(pl.multiple_of(b * 16, 16), 16)
        dn = total2[at, :].astype(F32) + dn_kv[at, :]
        dv, dg = norm_back(i.tokens[at, :].astype(F32), i.gains[0:1, :], dn)
        acc[0] += dg
        o.grad_tokens[at, :] = d_mid[at, :] + dv

    for g in range(3):
        gt[g : g + 1, :] = jnp.sum(acc[g], axis=0, keepdims=True)
    gt[3:4, :] = i.dg3[...]
    last = gt[...].T
    heads_t = hg[...].T
    tail[:, 2 * HD :] = last.astype(BF)
    for f in range(4):
        tail[288 * f : 288 * f + 64, 2 * HD :] = (
            last[288 * f : 288 * f + 64] + heads_t[64 * f : 64 * f + 64]
        ).astype(BF)
    rkv.one()
    roq.four()
    gate.fiveb()
    up.five()
    rkv.two()
    roq.fourb()
    down.six()
    rkv.three()
    up.fiveb()
    roq.five()
    rkv.four()
    rkv.fourb()
    roq.fiveb()
    gate.six()
    rkv.five()
    rkv.fiveb()
    up.six()
    roq.six()
    rkv.six()
    for d in range(8):
        for e in (1, 2, 3):
            key_copy(p.c, d, e).wait_send()
    for d in range(1, 8):
        value_copy(p.c, d).wait_send()
    for copy in kv2 + keys_far + values_far + gate.c1 + up.c1 + roq.c1 + rkv.c1:
        copy.wait_send()


def zsum_buffers(share):
    return [pltpu.VMEM((3, share, 1152), BF)] + sems(3) + sems(3)


def back_call(ins, cid):
    scratch = (
        [pltpu.VMEM(a.shape, a.dtype) for a in ins]
        + [pltpu.SemaphoreType.DMA((len(ins),))]
        + [pltpu.VMEM((256, 1152), BF), pltpu.VMEM((256, 1), F32)]
        + zsum_buffers(32) * 2
        + [pltpu.VMEM((256, 1152), BF)]
        + zsum_buffers(64)
        + [
            pltpu.VMEM((16, HD), BF),
            pltpu.VMEM((3, 16, HD), BF),
            pltpu.VMEM((256, 1152), F32),
            pltpu.VMEM((256, 1152), BF),
            pltpu.VMEM((256, HD), BF),
            pltpu.VMEM((256, 1), F32),
            pltpu.VMEM((256, HD), F32),
            pltpu.VMEM((8, 256, 2 * HD), BF),
            pltpu.VMEM((3, 8, 64, HD), BF),
            pltpu.VMEM((7, 256, HD), BF),
            pltpu.VMEM((8, 64, HD), BF),
            pltpu.VMEM((256, HD), BF),
            pltpu.VMEM((7, 64, HD), BF),
            pltpu.VMEM((3, 64, HD), BF),
            pltpu.VMEM((256, 2 * HD), BF),
            pltpu.VMEM((256, 1152), F32),
            pltpu.VMEM((4, 16, 1152), F32),
            pltpu.VMEM((128, 1152), F32),
            pltpu.VMEM((128, HD), F32),
            pltpu.VMEM((1152, 512), BF),
            pltpu.VMEM((1152, 640), BF),
        ]
        + sems(24)
        + sems(7)
        + sems(7)
        + sems(3)
        + sems(3)
        + sems(3)
        + reduce_buffers(1728, 896, True) * 2
        + reduce_buffers(1728, 896, False)
        + reduce_buffers(512, 256, False)
        + reduce_buffers(640, 384, False)
    )
    shapes = [((256, 1152), F32)] + [((288, n), BF) for n in (1728, 1728, 1728, 256, 256, 256, 256, 128)]
    return pl.pallas_call(
        back_kernel,
        out_shape=[jax.ShapeDtypeStruct(*shape) for shape in shapes],
        in_specs=[HB] * len(ins),
        out_specs=[VM] * len(shapes),
        scratch_shapes=scratch,
        compiler_params=params(cid, 62),
        name="backward",
    )(*ins)


class ForeIn(NamedTuple):
    tokens: Any
    cot: Any
    w_query: Any
    w_key: Any
    w_value: Any
    w_out: Any
    scales: Any
    head_scales: Any
    w_gate: Any
    w_up: Any
    w_down: Any
    cosine: Any
    sine: Any
    key_pos: Any

class ForeOut(NamedTuple):
    out: Any
    small: Any
    gains: Any
    heads: Any
    x: Any
    d_ffn_t: Any
    hidden: Any
    normed2_t: Any
    d_gate: Any
    d_up: Any
    middle: Any
    branch: Any
    dg3: Any
    attn: Any
    attn_low: Any
    lse: Any
    queries: Any
    kv: Any
    normed_t: Any
    q_proj: Any
    k_proj: Any

TILES = [(c0, min(c0 + 256, 1728)) for c0 in range(0, 1728, 256)]


def turn(v, cosine, sine):
    v1, v2 = v[:, :128], v[:, 128:]
    return jnp.concatenate([v1 * cosine - v2 * sine, v2 * cosine + v1 * sine], axis=1)


def transpose_into(dst, src):
    for c0 in range(0, 1152, 128):
        dst[c0 : c0 + 128, :] = src[:, c0 : c0 + 128].astype(F32).T.astype(BF)


def fore_kernel(*refs):
    n_in, n_out = len(ForeIn._fields), len(ForeOut._fields)
    i = ForeIn(*refs[:n_in])
    rest = list(refs[n_in + n_out :])

    def take(n):
        got = rest[:n]
        del rest[:n]
        return got

    o = ForeOut(*take(n_out))
    leaving = take(1)[0]
    leave = ForeOut(
        *[
            pltpu.make_async_copy(o[n], refs[n_in + n], leaving.at[n])
            for n in range(n_out)
        ]
    )
    p = Place()
    scale = HD ** (-0.5)
    w_gate, w_up, w_down, act, slope, normed, d_ffn, probs, head_cols, accg = take(10)
    local, gs, gr, ks, kr, vs, vr, fs, fr = take(9)
    total1, total2 = take(2)
    z1, z2 = take(10), take(10)
    part, pack, rows_up, own_pos = take(4)
    small = o.small
    halves = [(h, slice(128 * h, 128 * h + 128)) for h in (0, 1)]
    firsts = [ZSum(p, part, total1, 128 * h, *z1[5 * h : 5 * h + 5]) for h in (0, 1)]
    seconds = [ZSum(p, part, total2, 128 * h, *z2[5 * h : 5 * h + 5]) for h in (0, 1)]
    kv = o.kv
    gathers = [
        Gather(p, src, dst, local.at[j], gs, gr, 6 * j, 0 < j < 4)
        for j, (src, dst) in enumerate(
            [
                (pack.at[:, pl.ds(0, 896)], small.at[:, pl.ds(0, 896)]),
                (i.w_gate, w_gate),
                (i.w_up, w_up),
                (i.w_down, w_down),
                (pack.at[:, pl.ds(896, 256)], small.at[:, pl.ds(896, 256)]),
            ]
        )
    ]
    g_small, g_gate, g_up, g_down, g_out = gathers

    for ref, c0 in ((i.w_query, 0), (i.w_key, 256), (i.w_value, 512), (i.w_out, 896)):
        pack[:, c0 : c0 + 256] = ref[...]
    rows_up[...] = jnp.zeros_like(rows_up)
    rows_up[0:4, 0:288] = i.scales[...].astype(F32)
    rows_up[4:6, 0:64] = i.head_scales[...].astype(F32)
    pack[:, 768:896] = rows_up[...].T[:288, :].astype(BF)
    own_pos[...] = jnp.broadcast_to(i.key_pos[p.c], (8, 256)).T[:, 0:1]
    greet([p.sib(), p.dy(1), p.dy(3)] + [p.dc(d) for d in range(1, 8)] + [p.dz(d) for d in (1, 2, 3)])
    g_small.start()
    g_small.start_far()
    g_out.start()
    g_out.start_far()
    g_gate.start()
    g_up.start()
    g_down.start()
    accg[...] = jnp.zeros_like(accg)
    g_small.forward()
    g_gate.start_far()
    g_small.finish()

    o.gains[...] = small[:, 768:896].astype(F32).T[:8, :]
    for f in range(4):
        head_cols[64 * f : 64 * f + 64, :] = small[288 * f : 288 * f + 64, 768:896].astype(F32)
    o.heads[...] = head_cols[...].T[:8, :]
    leave.gains.start()
    leave.heads.start()

    @pl.loop(0, 16, unroll=4)
    def _(b):
        at = pl.ds(pl.multiple_of(b * 16, 16), 16)
        normed[at, :] = normalize(i.tokens[at, :].astype(F32), o.gains[0:1, :]).astype(BF)

    o.q_proj[...] = plain(normed[...], small[:, :256])
    o.k_proj[...] = plain(normed[...], small[:, 256:512])
    kv[p.c, :, HD:] = plain(normed[...], small[:, 512:768]).astype(BF)

    quarter = pl.ds(pl.multiple_of(p.z * 64, 64), 64)
    sent = [
        send(
            kv.at[p.c, quarter, pl.ds(HD, HD)],
            kv.at[p.c, quarter, pl.ds(HD, HD)],
            vs.at[d - 1],
            vr.at[d - 1],
            p.dc(d),
        )
        for d in range(1, 8)
    ]

    @pl.loop(0, 4)
    def _(b):
        at = pl.ds(pl.multiple_of(b * 64, 64), 64)
        n = normalize(o.k_proj[at, :], o.heads[5:6, :])
        kv[p.c, at, :HD] = turn(n, i.cosine[at, :], i.sine[at, :]).astype(BF)

    keys = kv.at[p.c, :, pl.ds(0, HD)]
    sent_k = [send(keys, keys, ks.at[d - 1], kr.at[d - 1], p.dc(d)) for d in range(1, 8)]

    @pl.loop(0, 4)
    def _(b):
        at = pl.ds(pl.multiple_of(b * 64, 64), 64)
        n = normalize(o.q_proj[at, :], o.heads[4:5, :])
        o.queries[at, :] = turn(n, i.cosine[at, :], i.sine[at, :]).astype(BF)

    g_out.forward()
    g_gate.across()
    g_up.start_far()
    for copy in sent:
        copy.wait_recv()
    sent_z = []
    for d in range(8):
        block = kv.at[(p.c + 8 - d) % 8, quarter, pl.ds(HD, HD)]
        if d == 0:
            continue
        sent_z += [
            send(block, block, fs.at[3 * d + e - 1], fr.at[3 * d + e - 1], p.dz(e))
            for e in (2, 1, 3)
        ]
    transpose_into(o.normed_t, normed)
    for copy in (leave.normed_t, leave.queries, leave.q_proj, leave.k_proj):
        copy.start()
    for copy in sent_k:
        copy.wait_recv()
    g_gate.forward()
    g_down.start_far()

    @pl.loop(0, 4)
    def _(b):
        at = pl.ds(pl.multiple_of(b * 64, 64), 64)
        query = o.queries[at, :]
        seen = [i.key_pos[kb] <= own_pos[at, :] for kb in range(8)]
        scores = [against(query, kv[kb, :, :HD]) * scale for kb in range(8)]
        top = jnp.max(jnp.where(seen[0], scores[0], -1e30), axis=-1, keepdims=True)
        for kb in range(1, 8):
            top = jnp.maximum(
                top, jnp.max(jnp.where(seen[kb], scores[kb], -1e30), axis=-1, keepdims=True)
            )
        scores = [jnp.where(seen[kb], jnp.exp(scores[kb] - top), 0.0) for kb in range(8)]
        total = jnp.sum(scores[0], axis=-1, keepdims=True)
        for kb in range(1, 8):
            total = total + jnp.sum(scores[kb], axis=-1, keepdims=True)
        o.lse[at, :] = top + jnp.log(total)
        share = 1.0 / total
        for kb in range(8):
            probs[kb, at, :] = (scores[kb] * share).astype(BF)

    g_up.across()
    g_out.finish()
    leave.small.start()
    for copy in sent_z:
        copy.wait_recv()
    attn = plain(probs[0], kv[0, :, HD:])
    for kb in range(1, 8):
        attn = attn + plain(probs[kb], kv[kb, :, HD:])
    o.attn[...] = attn
    attn_low = attn.astype(BF)
    o.attn_low[...] = attn_low
    for copy in (leave.kv, leave.lse, leave.attn, leave.attn_low):
        copy.start()
    for h, rows in halves:
        part[rows, :] = against(attn_low[rows], small[:, 896:]).astype(BF)
        firsts[h].start()
    g_up.forward()
    g_down.across()
    for half in firsts:
        half.middle()
    g_gate.finish()

    def middle_rows(b):
        at = pl.ds(pl.multiple_of(b * 16, 16), 16)
        branch = total1[at, :]
        o.branch[at, :] = branch
        middle = i.tokens[at, :].astype(F32) + normalize(
            branch.astype(F32), o.gains[1:2, :]
        )
        o.middle[at, :] = middle
        normed[at, :] = normalize(middle, o.gains[2:3, :]).astype(BF)

    for h, rows in halves:
        firsts[h].finish()
        pl.loop(8 * h, 8 * h + 8, unroll=4)(middle_rows)
    g_up.finish()
    leave.branch.start()
    leave.middle.start()
    for c0, c1 in TILES:
        gate = plain(normed[...], w_gate[:, c0:c1])
        up = plain(normed[...], w_up[:, c0:c1])
        bend = jnp.tanh(0.7978845608028654 * (gate + 0.044715 * gate * gate * gate))
        gelu = 0.5 * gate * (1.0 + bend)
        o.hidden[:, c0:c1] = (gelu * up).astype(BF)
        act[:, c0:c1] = gelu
        rise = 0.7978845608028654 * (1.0 + 0.134145 * gate * gate)
        slope[:, c0:c1] = up * (0.5 * (1.0 + bend) + 0.5 * gate * (1.0 - bend * bend) * rise)
    leave.hidden.start()
    g_down.forward()
    g_down.finish()
    for h, rows in halves:
        for c0 in range(0, 1152, 384):
            part[rows, c0 : c0 + 384] = against(
                o.hidden[rows, :], w_down[c0 : c0 + 384, :]
            ).astype(BF)
        seconds[h].start()
    transpose_into(o.normed2_t, normed)
    leave.normed2_t.start()
    for half in seconds:
        half.middle()

    def last_rows(b):
        at = pl.ds(pl.multiple_of(b * 16, 16), 16)
        ffn = total2[at, :].astype(F32)
        o.out[at, :] = (o.middle[at, :] + normalize(ffn, o.gains[3:4, :])).astype(BF)
        dv, dg = norm_back(ffn, o.gains[3:4, :], i.cot[at, :].astype(F32))
        accg[...] += dg
        d_ffn[at, :] = dv.astype(BF)

    for h, rows in halves:
        seconds[h].finish()
        pl.loop(8 * h, 8 * h + 8, unroll=4)(last_rows)
    o.dg3[...] = jnp.sum(accg[...], axis=0, keepdims=True)
    transpose_into(o.d_ffn_t, d_ffn)
    for copy in (leave.out, leave.dg3, leave.d_ffn_t):
        copy.start()
    for c0, c1 in TILES:
        d_hidden = plain(d_ffn[...], w_down[:, c0:c1])
        o.d_up[:, c0:c1] = (d_hidden * act[:, c0:c1]).astype(BF)
        o.d_gate[:, c0:c1] = (d_hidden * slope[:, c0:c1]).astype(BF)
    leave.d_up.start()
    leave.d_gate.start()
    for c0 in range(0, 1152, 384):
        o.x[:, c0 : c0 + 384] = (
            against(o.d_gate[...], w_gate[c0 : c0 + 384, :])
            + against(o.d_up[...], w_up[c0 : c0 + 384, :])
        ).astype(BF)
    leave.x.start()
    for copy in leave:
        copy.wait()
    for copy in sent + sent_k + sent_z:
        copy.wait_send()


def fore_call(ins, cid):
    shapes = ForeOut(
        out=((256, 1152), BF),
        small=((1152, 1152), BF),
        gains=((8, 1152), F32),
        heads=((8, 256), F32),
        x=((256, 1152), BF),
        d_ffn_t=((1152, 256), BF),
        hidden=((256, 1728), BF),
        normed2_t=((1152, 256), BF),
        d_gate=((256, 1728), BF),
        d_up=((256, 1728), BF),
        middle=((256, 1152), F32),
        branch=((256, 1152), BF),
        dg3=((1, 1152), F32),
        attn=((256, 256), F32),
        attn_low=((256, 256), BF),
        lse=((256, 1), F32),
        queries=((256, 256), BF),
        kv=((8, 256, 512), BF),
        normed_t=((1152, 256), BF),
        q_proj=((256, 256), F32),
        k_proj=((256, 256), F32),
    )
    scratch = (
        [pltpu.VMEM(*shape) for shape in shapes]
        + [pltpu.SemaphoreType.DMA((len(shapes),))]
        + [pltpu.VMEM((1152, 1728), BF)] * 3
        + [
            pltpu.VMEM((256, 1728), F32),
            pltpu.VMEM((256, 1728), F32),
            pltpu.VMEM((256, 1152), BF),
            pltpu.VMEM((256, 1152), BF),
            pltpu.VMEM((8, 256, 256), BF),
            pltpu.VMEM((256, 128), F32),
            pltpu.VMEM((16, 1152), F32),
            pltpu.SemaphoreType.DMA((5,)),
        ]
        + sems(30)
        + sems(7)
        + sems(7)
        + sems(24)
        + [pltpu.VMEM((256, 1152), BF)] * 2
        + zsum_buffers(32) * 4
        + [pltpu.VMEM((256, 1152), BF), pltpu.VMEM((288, 1152), BF)]
        + [pltpu.VMEM((128, 384), F32), pltpu.VMEM((256, 1), F32)]
    )
    done = pl.pallas_call(
        fore_kernel,
        out_shape=[jax.ShapeDtypeStruct(*shape) for shape in shapes],
        in_specs=[HB if a.shape == (288, 1728) else VM for a in ins],
        out_specs=[HB] * len(shapes),
        scratch_shapes=scratch,
        compiler_params=params(cid, 62),
        name="forward",
    )(*ins)
    return ForeOut(*done)


def final_kernel(*refs):
    ins, outs = refs[:10], refs[10:21]
    held, wide, (rows_ref, heads_ref, s_in, s_out) = refs[21:31], refs[31:38], refs[38:]
    loads = [pltpu.make_async_copy(ins[n], held[n], s_in.at[n]) for n in range(10)]
    for copy in loads:
        copy.start()
    stores = []
    for n in range(9):
        loads[n].wait()
        if n > 1:
            wide[n - 2][...] = held[n][...].astype(F32)
        copy = pltpu.make_async_copy(held[n] if n < 2 else wide[n - 2], outs[n], s_out.at[n])
        copy.start()
        stores.append(copy)
    loads[9].wait()
    columns = held[9][...].astype(F32).T
    rows_ref[...] = columns[:4, :]
    heads_ref[...] = columns[4:6, :64]
    for n, ref in ((9, rows_ref), (10, heads_ref)):
        copy = pltpu.make_async_copy(ref, outs[n], s_out.at[n])
        copy.start()
        stores.append(copy)
    for copy in stores:
        copy.wait()


def final_call(*ins):
    grads = [a.shape for a in ins[2:9]]
    shapes = [ins[0].shape, ins[1].shape] + grads + [(4, 288), (2, 64)]
    any_space = pl.BlockSpec(memory_space=pl.ANY)
    return pl.pallas_call(
        final_kernel,
        out_shape=[
            jax.ShapeDtypeStruct(shape, BF if n == 0 else F32) for n, shape in enumerate(shapes)
        ],
        in_specs=[any_space] * 10,
        out_specs=[any_space] * 11,
        scratch_shapes=[pltpu.VMEM(a.shape, a.dtype) for a in ins]
        + [pltpu.VMEM(shape, F32) for shape in grads]
        + [
            pltpu.VMEM((4, 288), F32),
            pltpu.VMEM((2, 64), F32),
            pltpu.SemaphoreType.DMA((10,)),
            pltpu.SemaphoreType.DMA((11,)),
        ],
        compiler_params=pltpu.CompilerParams(vmem_limit_bytes=62 * 2**20),
        name="final",
    )(*ins)


def per_device(
    tokens,
    block_order,
    cotangent,
    w_query,
    w_key,
    w_value,
    w_out,
    w_gate,
    w_up,
    w_down,
    gains,
    head_gains,
):
    _, rows, width = tokens.shape
    cycle_index = lax.axis_index("context")
    span = rows // 2
    seq_len = rows * 8

    offsets = jnp.arange(seq_len, dtype=jnp.int32)
    key_pos = (jnp.repeat(block_order, span, axis=1) * span + (offsets % span)[None, :])[0]
    query_pos = lax.dynamic_slice_in_dim(key_pos, cycle_index * rows, rows, 0)
    cosine, sine = tables(query_pos)
    ins = ForeIn(
        tokens=tokens[0],
        cot=cotangent[0],
        w_query=w_query,
        w_key=w_key,
        w_value=w_value,
        w_out=w_out.T,
        scales=gains,
        head_scales=head_gains,
        w_gate=w_gate,
        w_up=w_up,
        w_down=w_down.T,
        cosine=cosine,
        sine=sine,
        key_pos=key_pos.astype(F32).reshape(8, 1, rows),
    )
    held = fore_call(ins, 1)
    grad_tokens, sum_down, sum_gate, sum_up, sum_q, sum_o, sum_k, sum_v, last = back_call(
        BackIn(
            x=held.x,
            d_ffn_t=held.d_ffn_t,
            hidden=held.hidden,
            normed2_t=held.normed2_t,
            d_gate=held.d_gate,
            d_up=held.d_up,
            middle=held.middle,
            branch=held.branch,
            cot=ins.cot,
            tokens=ins.tokens,
            gains=held.gains,
            dg3=held.dg3,
            attn=held.attn,
            attn_low=held.attn_low,
            lse=held.lse,
            queries=held.queries,
            kv=held.kv,
            key_pos=ins.key_pos,
            small=held.small,
            normed_t=held.normed_t,
            q_proj=held.q_proj,
            k_proj=held.k_proj,
            heads=held.heads,
            cosine=ins.cosine,
            sine=ins.sine,
        ),
        2,
    )
    done = final_call(
        held.out, grad_tokens, sum_gate, sum_up, sum_down, sum_q, sum_k, sum_v, sum_o, last
    )
    result, d_tokens, d_gate, d_up, d_down, d_q, d_k, d_v, d_o, d_gains, d_heads = done
    return (
        result[None],
        d_tokens[None],
        d_q,
        d_k,
        d_v,
        d_o.T,
        d_gate,
        d_up,
        d_down.T,
        d_gains,
        d_heads,
    )


def solution(mesh):
    in_specs = (
        P("fsdp", "context", None),
        P("fsdp", None),
        P("fsdp", "context", None),
        P("fsdp", "tensor"),
        P("fsdp", None),
        P("fsdp", None),
        P("tensor", "fsdp"),
        P("fsdp", "tensor"),
        P("fsdp", "tensor"),
        P("tensor", "fsdp"),
        P(None, "fsdp"),
        P(None, "fsdp"),
    )
    out_specs = (
        P("fsdp", "context", None),
        P("fsdp", "context", None),
        P("fsdp", "tensor"),
        P("fsdp", None),
        P("fsdp", None),
        P("tensor", "fsdp"),
        P("fsdp", "tensor"),
        P("fsdp", "tensor"),
        P("tensor", "fsdp"),
        P(None, "fsdp"),
        P(None, "fsdp"),
    )
    return jax.shard_map(
        per_device, mesh=mesh, in_specs=in_specs, out_specs=out_specs, check_vma=False
    )
```
